128 devices in a mesh: row: 8 (over y, x_lo), col: 8 (over z, x_hi), panel: 2 (over core).
Axes of the slice: x: 4 (x_hi: 2, x_lo: 2; x = x_hi * 2 + x_lo), y: 4, z: 4, core: 2. Of those that a mesh axis runs over, the one named last changes fastest.
Arguments:
- basis_values: bfloat16 [2048, 2048, 128], P(('row', 'col', 'panel')), may hold values from -6 to 6
- potential: float32 [262144], P(('row', 'col', 'panel')), may hold values from -0.0009765625 to 0.0009765625
- pair_atoms: int32 [2, 16384], P(None, ('row', 'col', 'panel')), may hold values from 0 to 15
- target_device: int32 [16384, 1], P(('row', 'col', 'panel')), may hold values from 0 to 127; in each aligned block of 128 rows (0 to 127, 128 to 255, ...) at most 2 rows name the same one
- target_block: int32 [16384], P(('row', 'col', 'panel')), may hold values from 0 to 1
- density: bfloat16 [2048, 2048], P('row', 'col'), may hold values from -0.21875 to 0.21875
- density_mask: int32 [16, 16], P('row', 'col'), may hold values 0 or 1
- inverse_intersection: bfloat16 [2048, 4096], P('row', 'col'), may hold values from -6 to 6
- inverse_mask: int32 [16, 32], P('row', 'col'), may hold values 0 or 1
Outputs:
- gradient: float32 [2048, 4096], P('row', ('col', 'panel'))
The draws below stay inside these ranges and needn't reach their ends.
Inputs may be any that keep to these rules, and one draw needn't show every extreme that they name: `target_device`: among the 128 rows of one device no owner appears more than 2 times.
All inputs are finite; a program needn't handle non-finite values. No bound on the sum of `density_mask` or of `inverse_mask` on one device may be relied on, other than what follows from the above.
Results may differ from the reference program's by a relative error of at most 0.0058.
Values may be sent and summed in bfloat16 or wider, within the bound.
A program may use at most 128 MiB of HBM per device.

```python
import math
import jax
import jax.numpy as jnp
import numpy as np
from jax import lax

BS = 128
TB = 2
GP = 2048
NA = 16
PART_DEV = 128
NB = 16
PW = 4096
PARTS_SIZE = 16384
CAP = 2
N_ROW = 8
N_COL = 8
N_PANEL = 2
DEVICES = 128


def set_ends(values, stream_key, low, largest):
    dims = values.shape
    place = [jax.random.randint(jax.random.fold_in(stream_key, axis), (), 0, dims[axis]) for axis in range(len(dims))]
    values = values.at[tuple(place)].set(low)
    longest = dims.index(max(dims))
    place[longest] = (place[longest] + 1) % dims[longest]
    return values.at[tuple(place)].set(largest)


def level_of(own_key, shape, cuts, smallest, high):
    level = 1.0
    for dim, blocks in cuts:
        steps = jax.random.uniform(jax.random.fold_in(jax.random.fold_in(own_key, 6), dim), (blocks,), jnp.float32, smallest / len(cuts), high / len(cuts))
        level = level * jnp.repeat(jnp.exp(steps), shape[dim] // blocks).reshape((-1,) + (1,) * (len(shape) - 1 - dim))
    return level


def assign_block(rng, own, number, rows, count, top, limit, skew):
    ranking = jax.random.permutation(rng, count)
    crowded, usual = load_shares(count, rows * top, limit, skew, True), load_shares(count, rows * top, limit, skew, False)
    places = jnp.arange(count)

    def named(sizes, turn):
        used = int((sizes > 0).sum())
        fixed = max(1, used // 4)
        shifted = fixed + (places - fixed + turn * (used - fixed)) % max(1, count - fixed)
        return jnp.zeros((count,), jnp.int32).at[ranking[jnp.where(places < fixed, places, shifted)]].set(jnp.asarray(sizes, jnp.int32))

    sizes = jnp.where(number % 4 == 0, named(crowded, number // 4), named(usual, number - number // 4 - 1))
    mixed = jax.random.permutation(jax.random.fold_in(own, 3), count)
    giver, sink = mixed[0:count // 2 * 2:2], mixed[1:count // 2 * 2:2]
    slack = jnp.minimum(sizes[giver] - 1, limit - sizes[sink]) // 2
    slack = jnp.where((giver == ranking[0]) | (sink == ranking[0]) | (sizes[sink] == 0), 0, jnp.maximum(slack, 0))
    shifted = jax.random.randint(jax.random.fold_in(own, 4), (count // 2,), 0, 1 << 20) % (slack + 1)
    sizes = sizes.at[giver].add(-shifted).at[sink].add(shifted)
    members = jnp.searchsorted(jnp.cumsum(sizes), jnp.arange(rows * top), side="right").astype(jnp.int32)
    listing = members.reshape(top, rows).T
    listing = listing[jax.random.permutation(jax.random.fold_in(own, 1), rows)]
    turn = jax.random.randint(jax.random.fold_in(own, 2), (rows, 1), 0, top)
    return jnp.take_along_axis(listing, (jnp.arange(top)[None, :] + turn) % top, axis=1)


def load_shares(count, total, limit, lean, full):
    loads = [(1 << 20) // math.isqrt(grade ** lean) + 1 for grade in range(1, count + 1)]
    largest = limit if full else min(limit, max(-(-total // count), total * loads[0] // sum(loads)))
    least = 1 if total - largest >= count - 1 else 0
    counts, rest = [largest] + [least] * (count - 1), total - largest - least * (count - 1)
    while rest > 0:
        free = [i for i in range(1, count) if counts[i] < largest] or [i for i in range(1, count) if counts[i] < limit]
        mass, left = sum([loads[i] for i in free]), rest
        for i in free:
            more = min(limit - counts[i], max(1, left * loads[i] // mass), rest)
            counts[i] = counts[i] + more
            rest = rest - more
    return np.array(counts)


def gaussian(own_key, shape, scale, reach, split=(), kind=jnp.bfloat16):
    level = level_of(own_key, shape, split, -0.22, 0.18) if split else 1.0
    drawn = jax.random.normal(own_key, shape, jnp.float32) * scale * level
    return jnp.minimum(jnp.maximum(drawn, -reach), reach).astype(kind)


def setup_inputs(seed: int = 0) -> dict:
    streams_of = jax.random.split(jax.random.key(seed), 10)
    basis_values = gaussian(streams_of[0], (NA * DEVICES, GP, BS), 1.0, 6.0, ((0, 128),))
    potential = gaussian(streams_of[1], (GP * DEVICES,), (GP * NB * BS * 8) ** -0.5, 0.0009765625, ((0, 128),), jnp.float32)
    pair_atoms = set_ends(jax.random.randint(streams_of[2], (2, PARTS_SIZE), 0, NA), jax.random.fold_in(streams_of[2], 1), 0, NA - 1).astype(jnp.int32)
    target_device_keys = jax.random.split(jax.random.fold_in(streams_of[3], 1), PARTS_SIZE // PART_DEV)
    target_device_turns = jax.random.permutation(jax.random.fold_in(streams_of[3], 3), PARTS_SIZE // PART_DEV)
    target_device = jax.vmap(lambda own, number: assign_block(jax.random.fold_in(streams_of[3], 2), own, number, PART_DEV, DEVICES, 1, CAP, 2))(target_device_keys, target_device_turns).reshape((PARTS_SIZE, 1))
    target_block = set_ends(jax.random.randint(streams_of[4], (PARTS_SIZE,), 0, TB * TB // N_PANEL), jax.random.fold_in(streams_of[4], 1), 0, (TB * TB // N_PANEL) - 1).astype(jnp.int32)
    density = gaussian(streams_of[5], (NB * BS, NB * BS), (NB * BS // 3) ** -0.5, 0.21875, ((0, 8), (1, 8)))
    density_mask = set_ends((jax.random.randint(streams_of[6], (NB, NB), 0, 3) < 1).astype(jnp.int32), jax.random.fold_in(streams_of[6], 1), 0, 1)
    inverse_intersection = gaussian(streams_of[7], (NB * BS, PW), 1.0, 6.0, ((0, 8), (1, 8)))
    inverse_mask = set_ends((jax.random.randint(streams_of[8], (NB, PW // BS), 0, 2) < 1).astype(jnp.int32), jax.random.fold_in(streams_of[8], 1), 0, 1)
    return {"basis_values": basis_values, "potential": potential, "pair_atoms": pair_atoms, "target_device": target_device, "target_block": target_block, "density": density, "density_mask": density_mask, "inverse_intersection": inverse_intersection, "inverse_mask": inverse_mask}


def masked_blocks(matrix, block_mask):
    mask_rows, mask_cols = block_mask.shape
    shaped = matrix.reshape(mask_rows, BS, mask_cols, BS)
    factor = block_mask.astype(matrix.dtype)[:, None, :, None]
    return (shaped * factor).reshape(mask_rows * BS, mask_cols * BS)


def reference(basis_values, potential, pair_atoms, target_device, target_block, density, density_mask, inverse_intersection, inverse_mask):
    regions = N_ROW * N_COL * N_PANEL
    half_rows = TB // N_PANEL
    basis = basis_values.reshape(regions, NA, GP, BS)
    weights = potential.reshape(regions, GP)
    left_ids = pair_atoms[0].reshape(regions, PART_DEV)
    right_ids = pair_atoms[1].reshape(regions, PART_DEV)
    owner = target_device[:, 0]
    owner_row = owner // (N_COL * N_PANEL)
    owner_col = (owner // N_PANEL) % N_COL
    owner_layer = owner % N_PANEL
    block_row = owner_row * TB + owner_layer * half_rows + target_block // TB
    block_col = owner_col * TB + target_block % TB
    block_ids = (block_row * NB + block_col).astype(jnp.int32).reshape(regions, PART_DEV)

    def integrate(summed, inputs):
        region_basis, region_weights, left_pick, right_pick, region_blocks = inputs
        weighted = (region_basis.astype(jnp.float32) * region_weights[None, :, None]).astype(jnp.bfloat16)
        left_rows = region_basis[left_pick].astype(jnp.float32)
        right_rows = weighted[right_pick].astype(jnp.float32)
        partials = jnp.einsum("pgi,pgj->pij", left_rows, right_rows).astype(jnp.bfloat16)
        return summed.at[region_blocks].add(partials.astype(jnp.float32)), None

    summed = jnp.zeros((NB * NB, BS, BS), jnp.float32)
    summed, unused = lax.scan(integrate, summed, (basis, weights, left_ids, right_ids, block_ids))
    hamiltonian = summed.reshape(NB, NB, BS, BS).transpose(0, 2, 1, 3).reshape(NB * BS, NB * BS).astype(jnp.bfloat16)
    density_used = masked_blocks(density, density_mask)
    inverse_used = masked_blocks(inverse_intersection, inverse_mask)
    panel_product = jnp.dot(density_used, inverse_used, preferred_element_type=jnp.float32).astype(jnp.bfloat16)
    return jnp.dot(hamiltonian, panel_product, preferred_element_type=jnp.float32)
```

```python
import functools

import jax
import jax.numpy as jnp
from jax import lax
from jax.experimental import pallas as pl
from jax.experimental.pallas import tpu as pltpu
from jax.sharding import PartitionSpec as P

ALL = ("row", "col", "panel")


def masked_blocks(matrix, block_mask, block_size):
    mask_rows, mask_cols = block_mask.shape
    shaped = matrix.reshape(mask_rows, block_size, mask_cols, block_size)
    factor = block_mask.astype(matrix.dtype)[:, None, :, None]
    return (shaped * factor).reshape(mask_rows * block_size, mask_cols * block_size)


SIZE = 128
SHARES = (48, 48, 32)
STARTS = (0, 48, 96)
ORDERS = (("x", "y", "z"), ("y", "z", "x"), ("z", "x", "y"))


def gram_kernel(first_ref, second_ref, weight_ref, basis_ref, out0, out1, out2, raw, left, right, blocks, column, sem):
    atoms, points, size = basis_ref.shape
    chunks = points // size

    def fetch(a):
        return pltpu.make_async_copy(basis_ref.at[a], raw.at[a], sem.at[a])

    for a in range(atoms):
        fetch(a).start()
    for k in range(chunks):
        spread = jnp.broadcast_to(weight_ref[k : k + 1, :], (size, size))
        column[k * size : (k + 1) * size, :] = spread.T
    blocks[atoms * atoms] = jnp.zeros((size, size), jnp.bfloat16)
    for a in range(atoms):
        fetch(a).wait()

        @pl.loop(0, chunks)
        def _(k):
            rows = pl.ds(pl.multiple_of(k * size, size), size)
            piece = raw[a, rows, :]
            left[pl.ds(a * size, size), rows] = piece.T
            scaled = piece.astype(jnp.float32) * column[rows, :]
            right[rows, pl.ds(a * size, size)] = scaled.astype(jnp.bfloat16)

    tall, wide = 4, 2

    @pl.loop(0, (atoms // tall) * (atoms // wide))
    def _(t):
        i, j = t // (atoms // wide), t % (atoms // wide)
        rows = pl.ds(pl.multiple_of(i * tall * size, tall * size), tall * size)
        cols = pl.ds(pl.multiple_of(j * wide * size, wide * size), wide * size)
        product = jnp.dot(left[rows, :], right[:, cols], preferred_element_type=jnp.float32)
        for u in range(tall):
            for v in range(wide):
                part = product[u * size : (u + 1) * size, v * size : (v + 1) * size]
                blocks[(i * tall + u) * atoms + j * wide + v] = part.astype(jnp.bfloat16)

    @pl.loop(0, first_ref.shape[0])
    def _(n):
        y, x_lo, z, x_hi, p, b = n // 64, n // 32 % 2, n // 8 % 4, n // 4 % 2, n // 2 % 2, n % 2
        at = {"x": x_hi * 2 + x_lo, "y": y, "z": z}
        total = blocks[first_ref[n]] + blocks[second_ref[n]]
        for out, order, start, share in zip((out0, out1, out2), ORDERS, STARTS, SHARES):
            d0, d1, d2 = (at[axis] for axis in order)
            out[p, d0, (d1 * 4 + d2) * 2 + b] = total[start : start + share, :]


def gram_blocks(first, second, weights, basis):
    atoms, points, size = basis.shape
    vmem = pl.BlockSpec(memory_space=pltpu.VMEM)
    smem = pl.BlockSpec(memory_space=pltpu.SMEM)
    return pl.pallas_call(
        gram_kernel,
        out_shape=[jax.ShapeDtypeStruct((2, 4, 32, share, size), jnp.bfloat16) for share in SHARES],
        in_specs=[smem, smem, vmem, pl.BlockSpec(memory_space=pl.ANY)],
        out_specs=[vmem] * 3,
        scratch_shapes=[
            pltpu.VMEM((atoms, points, size), jnp.bfloat16),
            pltpu.VMEM((atoms * size, points), jnp.bfloat16),
            pltpu.VMEM((points, atoms * size), jnp.bfloat16),
            pltpu.VMEM((atoms * atoms + 1, size, size), jnp.bfloat16),
            pltpu.VMEM((points, size), jnp.float32),
            pltpu.SemaphoreType.DMA((atoms,)),
        ],
        compiler_params=pltpu.CompilerParams(vmem_limit_bytes=56 << 20),
        cost_estimate=pl.CostEstimate(
            flops=2 * (atoms * size) ** 2 * points, bytes_accessed=20 << 20, transcendentals=0
        ),
    )(first, second, weights.reshape(-1, size), basis)


def place():
    row, col, core = (lax.axis_index(axis) for axis in ALL)
    return {"x": col % 2 * 2 + row % 2, "y": row // 2, "z": col // 2, "core": core}


def device_at(spot):
    return (spot["y"] * 2 + spot["x"] % 2, spot["z"] * 2 + spot["x"] // 2, spot["core"])


def moved(spot, axis, steps):
    return {**spot, axis: (spot[axis] + steps) % (2 if axis == "core" else 4)}


def reduce_kernel(
    in0, in1, in2, out_ref,
    own0, own1, own2, pair0, pair1, pair2,
    got10, got11, got12, one0, one1, one2,
    got20, got21, got22, two0, two1, two2,
    got30, got31, got32, row_buf,
    load_sem, pair_send, pair_recv, send_sem, recv_sem, gather_send, gather_recv, share_send, share_recv, out_sem,
):
    here = place()
    ins, own, pair = (in0, in1, in2), (own0, own1, own2), (pair0, pair1, pair2)
    sources = (own, (one0, one1, one2), (two0, two1, two2))
    lands = ((got10, got11, got12), (got20, got21, got22), (got30, got31, got32))
    partner = moved(here, "core", 1)
    mesh = pl.DeviceIdType.MESH

    peers = [partner]
    for axis in ("x", "y", "z"):
        peers += [moved(here, axis, d) for d in (1, 2, 3)]
    peers += [moved(moved(here, "x", 2), "z", d) for d in (1, 2, 3)]
    barrier = pltpu.get_barrier_semaphore()
    for peer in peers:
        pl.semaphore_signal(barrier, inc=1, device_id=device_at(peer), device_id_type=mesh)
    pl.semaphore_wait(barrier, len(peers))

    def load(k, d):
        q = (here[ORDERS[k][0]] + d) % 4
        return pltpu.make_async_copy(ins[k].at[here["core"], q], own[k].at[q], load_sem.at[k, d])

    def swap(k, d):
        q = (here[ORDERS[k][0]] + d) % 4
        return pltpu.make_async_remote_copy(
            ins[k].at[partner["core"], q], pair[k].at[q], pair_send.at[k, d], pair_recv.at[k, d],
            device_id=device_at(partner), device_id_type=mesh,
        )

    def pass_on(stage, k, d):
        axis = ORDERS[k][stage]
        return pltpu.make_async_remote_copy(
            sources[stage][k].at[(here[axis] + d) % 4], lands[stage][k].at[d - 1],
            send_sem.at[stage, k, d - 1], recv_sem.at[stage, k, d - 1],
            device_id=device_at(moved(here, axis, d)), device_id_type=mesh,
        )

    turns = (2, 1, 3, 0)
    for d in turns:
        for k in range(3):
            swap(k, d).start()
            load(k, d).start()
    for d in turns:
        for k in range(3):
            load(k, d).wait()
            swap(k, d).wait_recv()
            q = (here[ORDERS[k][0]] + d) % 4

            @pl.loop(0, 32)
            def _(n):
                own[k][q, n] = own[k][q, n] + pair[k][q, n]

            if d:
                pass_on(0, k, d).start()

    def total(stage, k, n):
        mine = sources[stage][k][here[ORDERS[k][stage]], n].astype(jnp.float32)
        for d in range(3):
            mine = mine + lands[stage][k][d, n].astype(jnp.float32)
        return mine.astype(jnp.bfloat16)

    for stage in (0, 1):
        later = sources[stage + 1]
        count = 8 if stage == 0 else 2
        for k in range(3):
            for d in (1, 2, 3):
                pass_on(stage, k, d).wait_recv()

            @pl.loop(0, 4)
            def _(q):
                for n in range(count):
                    later[k][q, n] = total(stage, k, q * count + n)

            for d in (2, 1, 3):
                pass_on(stage + 1, k, d).start()

    col = here["z"] * 2 + here["x"] // 2
    own_rows = pl.multiple_of(here["core"] * SIZE, SIZE)
    for k in range(3):
        for d in (1, 2, 3):
            pass_on(2, k, d).wait_recv()
        for b in range(2):
            row_buf[pl.ds(own_rows + STARTS[k], SHARES[k]), pl.ds(pl.multiple_of(col * 256 + b * SIZE, SIZE), SIZE)] = total(2, k, b)

    def tile(spot):
        c = spot["z"] * 2 + spot["x"] // 2
        return row_buf.at[pl.ds(own_rows, SIZE), pl.ds(pl.multiple_of(c * 256, 256), 256)]

    def spread(dz, dx):
        return pltpu.make_async_remote_copy(
            tile(here), tile(here), gather_send.at[dz * 2 + dx], gather_recv.at[dz * 2 + dx],
            device_id=device_at(moved(moved(here, "x", 2 * dx), "z", dz)), device_id_type=mesh,
        )

    def share(dz, dx):
        spot = moved(moved(here, "x", 2 * dx), "z", -dz)
        return pltpu.make_async_remote_copy(
            tile(spot), tile(spot), share_send.at[dz * 2 + dx], share_recv.at[dz * 2 + dx],
            device_id=device_at(partner), device_id_type=mesh,
        )

    steps = ((2, 1), (1, 1), (3, 1), (2, 0), (0, 1), (1, 0), (3, 0))
    for step in steps:
        spread(*step).start()
    share(0, 0).start()
    for step in steps[::-1]:
        spread(*step).wait_recv()
        share(*step).start()
    for step in ((0, 0),) + steps:
        share(*step).wait()
    for step in steps:
        spread(*step).wait_send()
    done = pltpu.make_async_copy(row_buf, out_ref, out_sem)
    done.start()
    for k in range(3):
        for d in turns:
            swap(k, d).wait_send()
        for stage in range(3):
            for d in (1, 2, 3):
                pass_on(stage, k, d).wait_send()
    done.wait()


def reduced_row(parts):
    def buffers(*lead):
        return [pltpu.VMEM((*lead, share, SIZE), jnp.bfloat16) for share in SHARES]

    dma = pltpu.SemaphoreType.DMA
    hbm = pl.BlockSpec(memory_space=pl.ANY)
    return pl.pallas_call(
        reduce_kernel,
        out_shape=jax.ShapeDtypeStruct((2 * SIZE, 16 * SIZE), jnp.bfloat16),
        in_specs=[hbm] * 3,
        out_specs=hbm,
        scratch_shapes=[
            *buffers(4, 32), *buffers(4, 32),
            *buffers(3, 32), *buffers(4, 8),
            *buffers(3, 8), *buffers(4, 2),
            *buffers(3, 2),
            pltpu.VMEM((2 * SIZE, 16 * SIZE), jnp.bfloat16),
            dma((3, 4)), dma((3, 4)), dma((3, 4)), dma((3, 3, 3)), dma((3, 3, 3)),
            dma((8,)), dma((8,)), dma((8,)), dma((8,)), dma,
        ],
        compiler_params=pltpu.CompilerParams(
            collective_id=0, has_side_effects=True, vmem_limit_bytes=58 << 20
        ),
        cost_estimate=pl.CostEstimate(flops=1 << 33, bytes_accessed=64 << 20, transcendentals=0),
    )(*parts)


def local(
    basis_values,
    potential,
    pair_atoms,
    target_device,
    target_block,
    density,
    density_mask,
    inverse_intersection,
    inverse_mask,
):
    atoms, _, size = basis_values.shape
    tile_blocks = density_mask.shape[0]
    devices = lax.axis_size(ALL)
    per_owner = tile_blocks * tile_blocks // lax.axis_size("panel")
    empty = atoms * atoms

    target = target_device[:, 0] * per_owner + target_block
    serial = jnp.arange(target.shape[0], dtype=jnp.int32)
    key = serial * empty + pair_atoms[0] * atoms + pair_atoms[1]
    hit = target[None, :] == jnp.arange(devices * per_owner, dtype=jnp.int32)[:, None]
    low = jnp.min(jnp.where(hit, key[None, :], 1 << 30), axis=1)
    high = jnp.max(jnp.where(hit, key[None, :], -1), axis=1)
    first = jnp.where(high >= 0, low % empty, empty)
    second = jnp.where(high > low, high % empty, empty)

    density_used = masked_blocks(density, density_mask, size)
    inverse_used = masked_blocks(inverse_intersection, inverse_mask, size)
    width = inverse_used.shape[1] // lax.axis_size("panel")
    own = lax.dynamic_slice_in_dim(inverse_used, lax.axis_index("panel") * width, width, 1)
    density_used, own, first = lax.optimization_barrier((density_used, own, first))
    p_rows = lax.all_gather(density_used, "col", axis=1, tiled=True)
    s_cols = lax.all_gather(own, "row", axis=0, tiled=True)
    parts = gram_blocks(first, second, potential, basis_values)
    product = jnp.dot(p_rows, s_cols, preferred_element_type=jnp.float32).astype(jnp.bfloat16)
    product, *parts = lax.optimization_barrier((product, *parts))
    x_cols = lax.all_gather(product, "row", axis=0, tiled=True)
    hamiltonian = reduced_row(parts)
    return jnp.dot(hamiltonian, x_cols, preferred_element_type=jnp.float32)


def solution(mesh):
    placed = (
        P(ALL, None, None),
        P(ALL),
        P(None, ALL),
        P(ALL, None),
        P(ALL),
        P("row", "col"),
        P("row", "col"),
        P("row", "col"),
        P("row", "col"),
    )
    return jax.shard_map(
        local, mesh=mesh, in_specs=placed, out_specs=P("row", ("col", "panel")), check_vma=False
    )
```

```python
import functools

import jax
import jax.numpy as jnp
from jax import lax
from jax.experimental import pallas as pl
from jax.experimental.pallas import tpu as pltpu
from jax.sharding import PartitionSpec as P

ALL = ("row", "col", "panel")


def masked_blocks(matrix, block_mask, block_size):
    mask_rows, mask_cols = block_mask.shape
    shaped = matrix.reshape(mask_rows, block_size, mask_cols, block_size)
    factor = block_mask.astype(matrix.dtype)[:, None, :, None]
    return (shaped * factor).reshape(mask_rows * block_size, mask_cols * block_size)


SIZE = 128
SHARES = (48, 48, 32)
STARTS = (0, 48, 96)
ORDERS = (("x", "y", "z"), ("y", "z", "x"), ("z", "x", "y"))


def place():
    row, col, core = (lax.axis_index(axis) for axis in ALL)
    return {"x": col % 2 * 2 + row % 2, "y": row // 2, "z": col // 2, "core": core}


def device_at(spot):
    return (spot["y"] * 2 + spot["x"] % 2, spot["z"] * 2 + spot["x"] // 2, spot["core"])


def moved(spot, axis, steps):
    return {**spot, axis: (spot[axis] + steps) % (2 if axis == "core" else 4)}


def tile_column(spot):
    return spot["z"] * 2 + spot["x"] // 2


def tile_row(spot):
    return spot["y"] * 2 + spot["x"] % 2


def in_row(spot, dz, dx):
    return moved(moved(spot, "x", 2 * dx), "z", dz)


def in_column(spot, dy, dx):
    return moved({**spot, "x": spot["x"] // 2 * 2 + (spot["x"] + dx) % 2}, "y", dy)


STEPS = ((2, 1), (1, 1), (3, 1), (2, 0), (0, 1), (1, 0), (3, 0))


def whole_kernel(
    first_ref, second_ref, weight_ref, basis_ref, density_ref, inverse_ref, out_ref,
    raw, left, right, blocks, column,
    own0, own1, own2, give0, give1, give2, pair0, pair1, pair2,
    relay0, relay1, relay2, near0, near1, near2, one0, one1, one2,
    got20, got21, got22, two0, two1, two2, got30, got31, got32,
    p_row, s_col, x_col, row_buf,
    fetch_sem, pair_send, pair_recv, relay_send, relay_recv, near_send, near_recv, send_sem, recv_sem,
    p_send, p_recv, s_send, s_recv, x_send, x_recv, gather_send, gather_recv, share_send, share_recv,
):
    here = place()
    own, give, pair = (own0, own1, own2), (give0, give1, give2), (pair0, pair1, pair2)
    relay, near, one = (relay0, relay1, relay2), (near0, near1, near2), (one0, one1, one2)
    two = (two0, two1, two2)
    sources, lands = (None, one, two), (None, (got20, got21, got22), (got30, got31, got32))
    partner = moved(here, "core", 1)
    mesh = pl.DeviceIdType.MESH
    atoms, points, size = basis_ref.shape
    chunks = points // size
    slots = raw.shape[0]

    def fetch(a):
        return pltpu.make_async_copy(basis_ref.at[a], raw.at[a % slots], fetch_sem.at[a])

    for a in range(slots):
        fetch(a).start()

    peers = [partner]
    for axis in ("x", "y", "z"):
        peers += [moved(here, axis, d) for d in (1, 2, 3)]
    peers += [in_row(here, d, 1) for d in (1, 2, 3)]
    peers += [in_column(here, d, 1) for d in (1, 2, 3)]
    barrier = pltpu.get_barrier_semaphore()
    for peer in peers:
        pl.semaphore_signal(barrier, inc=1, device_id=device_at(peer), device_id_type=mesh)

    for k in range(chunks):
        spread_row = jnp.broadcast_to(weight_ref[k : k + 1, :], (size, size))
        column[k * size : (k + 1) * size, :] = spread_row.T
    blocks[atoms * atoms] = jnp.zeros((size, size), jnp.bfloat16)

    def remote(src, dst, send, recv, spot):
        return pltpu.make_async_remote_copy(
            src_ref=src, dst_ref=dst, send_sem=send, recv_sem=recv,
            device_id=device_at(spot), device_id_type=mesh,
        )

    tile = 2 * size
    own_col = pl.ds(pl.multiple_of(tile_column(here) * tile, tile), tile)
    own_row = pl.ds(pl.multiple_of(tile_row(here) * tile, tile), tile)

    def send_p(dz, dx):
        at = dz * 2 + dx
        return remote(density_ref, p_row.at[:, own_col], p_send.at[at], p_recv.at[at], in_row(here, dz, dx))

    def send_s(dy, dx):
        at = dy * 2 + dx
        return remote(inverse_ref, s_col.at[own_row, :], s_send.at[at], s_recv.at[at], in_column(here, dy, dx))

    def send_x(dy, dx):
        at = dy * 2 + dx
        rows = x_col.at[own_row, :]
        return remote(rows, rows, x_send.at[at], x_recv.at[at], in_column(here, dy, dx))

    pl.semaphore_wait(barrier, len(peers))
    for step in STEPS:
        send_p(*step).start()
        send_s(*step).start()
    p_row[:, own_col] = density_ref[...]
    s_col[own_row, :] = inverse_ref[...]

    @pl.loop(0, atoms)
    def _(a):
        fetch(a).wait()
        cols = pl.ds(pl.multiple_of(a * size, size), size)
        for k in range(chunks):
            rows = pl.ds(k * size, size)
            piece = raw[a % slots, rows, :]
            left[cols, rows] = piece.T
            scaled = piece.astype(jnp.float32) * column[rows, :]
            right[rows, cols] = scaled.astype(jnp.bfloat16)

        @pl.when(a < atoms - slots)
        def _():
            fetch(a + slots).start()

    @pl.loop(0, atoms // 2)
    def _(j):
        cols = pl.ds(pl.multiple_of(j * 2 * size, 2 * size), 2 * size)
        product = jnp.dot(left[...], right[:, cols], preferred_element_type=jnp.float32)
        for u in range(atoms):
            for v in range(2):
                part = product[u * size : (u + 1) * size, v * size : (v + 1) * size]
                blocks[u * atoms + j * 2 + v] = part.astype(jnp.bfloat16)

    for step in STEPS:
        send_p(*step).wait_recv()
        send_s(*step).wait_recv()
    x_col[own_row, :] = jnp.dot(p_row[...], s_col[...], preferred_element_type=jnp.float32).astype(jnp.bfloat16)
    for step in STEPS:
        send_x(*step).start()

    def spot_of(k, d):
        return (here[ORDERS[k][0]] + d) % 4

    def assembled(k, q, m, g, core):
        at = dict(zip(ORDERS[k], (q, m, g // 2)))
        n = ((tile_row(at) * 8 + tile_column(at)) * 2 + core) * 2 + g % 2
        rows = pl.ds(STARTS[k], SHARES[k])
        return blocks[first_ref[n], rows, :] + blocks[second_ref[n], rows, :]

    def swap(k, d):
        q = spot_of(k, d)
        return remote(give[k].at[q], pair[k].at[q], pair_send.at[k, d], pair_recv.at[k, d], partner)

    def pass_relay(k, side):
        half = pl.ds(16 * side, 16)
        return remote(
            own[k].at[spot_of(k, 2), half], relay[k].at[side], relay_send.at[k, side], relay_recv.at[k, side],
            moved(here, ORDERS[k][0], 3 if side else 1),
        )

    def pass_near(k, side, part):
        half = pl.ds(16 * part, 16)
        d = 3 if side else 1
        return remote(
            own[k].at[spot_of(k, d), half], near[k].at[side, half],
            near_send.at[k, side, part], near_recv.at[k, side, part], moved(here, ORDERS[k][0], d),
        )

    def pass_on(stage, k, d):
        axis = ORDERS[k][stage]
        return remote(
            sources[stage][k].at[(here[axis] + d) % 4], lands[stage][k].at[d - 1],
            send_sem.at[stage - 1, k, d - 1], recv_sem.at[stage - 1, k, d - 1], moved(here, axis, d),
        )

    turns = (2, 1, 3, 0)
    for d in turns:
        for k in range(3):
            q = spot_of(k, d)

            @pl.loop(0, 4)
            def _(m):
                for g in range(8):
                    give[k][q, m * 8 + g] = assembled(k, q, m, g, partner["core"])

            swap(k, d).start()
    for d in turns:
        for k in range(3):
            q = spot_of(k, d)
            swap(k, d).wait_recv()

            @pl.loop(0, 4)
            def _(m):
                for g in range(8):
                    own[k][q, m * 8 + g] = assembled(k, q, m, g, here["core"]) + pair[k][q, m * 8 + g]

            if d == 2:
                pass_relay(k, 0).start()
                pass_relay(k, 1).start()
            if d == 1:
                pass_near(k, 0, 1).start()
            if d == 3:
                pass_near(k, 1, 0).start()
    for k in range(3):
        for side in range(2):
            q = spot_of(k, 3 if side else 1)
            pass_relay(k, side).wait_recv()

            @pl.loop(0, 4)
            def _(m):
                for g in range(4):
                    n = m * 4 + g
                    own[k][q, 16 * side + n] = own[k][q, 16 * side + n] + relay[k][side, n]

            pass_near(k, side, side).start()
    for k in range(3):
        q = spot_of(k, 0)
        for side in range(2):
            for part in range(2):
                pass_near(k, side, part).wait_recv()

        @pl.loop(0, 4)
        def _(m):
            for g in range(8):
                n = m * 8 + g
                total = own[k][q, n].astype(jnp.float32) + near[k][0, n].astype(jnp.float32)
                one[k][m, g] = (total + near[k][1, n].astype(jnp.float32)).astype(jnp.bfloat16)

        for d in (2, 1, 3):
            pass_on(1, k, d).start()

    def added(stage, k, n):
        mine = sources[stage][k][here[ORDERS[k][stage]], n].astype(jnp.float32)
        for d in range(3):
            mine = mine + lands[stage][k][d, n].astype(jnp.float32)
        return mine.astype(jnp.bfloat16)

    for k in range(3):
        for d in (1, 2, 3):
            pass_on(1, k, d).wait_recv()
        for q in range(4):
            for b in range(2):
                two[k][q, b] = added(1, k, q * 2 + b)
        for d in (2, 1, 3):
            pass_on(2, k, d).start()

    core_row = pl.multiple_of(here["core"] * size, size)
    for k in range(3):
        for d in (1, 2, 3):
            pass_on(2, k, d).wait_recv()
        for b in range(2):
            cols = pl.ds(pl.multiple_of(tile_column(here) * tile + b * size, size), size)
            row_buf[pl.ds(core_row + STARTS[k], SHARES[k]), cols] = added(2, k, b)

    def tile_of(spot):
        cols = pl.ds(pl.multiple_of(tile_column(spot) * tile, tile), tile)
        return row_buf.at[pl.ds(core_row, size), cols]

    def spread(dz, dx):
        at = dz * 2 + dx
        return remote(tile_of(here), tile_of(here), gather_send.at[at], gather_recv.at[at], in_row(here, dz, dx))

    def share(dz, dx):
        at = dz * 2 + dx
        from_there = tile_of(in_row(here, 4 - dz, dx))
        return remote(from_there, from_there, share_send.at[at], share_recv.at[at], partner)

    for step in STEPS:
        spread(*step).start()
    share(0, 0).start()
    for step in STEPS:
        send_x(*step).wait_recv()
    for step in STEPS[::-1]:
        spread(*step).wait_recv()
        share(*step).start()
    for step in ((0, 0),) + STEPS:
        share(*step).wait_recv()
    out_ref[...] = jnp.dot(row_buf[...], x_col[...], preferred_element_type=jnp.float32)

    for step in STEPS:
        for copy in (send_p, send_s, send_x, spread, share):
            copy(*step).wait_send()
    share(0, 0).wait_send()
    for k in range(3):
        for d in turns:
            swap(k, d).wait_send()
        for side in range(2):
            pass_relay(k, side).wait_send()
            for part in range(2):
                pass_near(k, side, part).wait_send()
        for stage in (1, 2):
            for d in (1, 2, 3):
                pass_on(stage, k, d).wait_send()


def gradient_tile(first, second, weights, basis, density, inverse):
    atoms, points, size = basis.shape
    depth = 16 * size

    def buffers(*lead):
        return [pltpu.VMEM((*lead, share, size), jnp.bfloat16) for share in SHARES]

    def plain(*shape):
        return pltpu.VMEM(shape, jnp.bfloat16)

    dma = pltpu.SemaphoreType.DMA
    vmem = pl.BlockSpec(memory_space=pltpu.VMEM)
    smem = pl.BlockSpec(memory_space=pltpu.SMEM)
    return pl.pallas_call(
        whole_kernel,
        out_shape=jax.ShapeDtypeStruct((2 * size, 2 * size), jnp.float32),
        in_specs=[smem, smem, vmem, pl.BlockSpec(memory_space=pl.ANY), vmem, vmem],
        out_specs=vmem,
        scratch_shapes=[
            plain(atoms // 2, points, size), plain(atoms * size, points), plain(points, atoms * size),
            plain(atoms * atoms + 1, size, size), pltpu.VMEM((points, size), jnp.float32),
            *buffers(4, 32), *buffers(4, 32), *buffers(4, 32),
            *buffers(2, 16), *buffers(2, 32), *buffers(4, 8),
            *buffers(3, 8), *buffers(4, 2), *buffers(3, 2),
            plain(2 * size, depth), plain(depth, 2 * size), plain(depth, 2 * size), plain(2 * size, depth),
            dma((atoms,)), dma((3, 4)), dma((3, 4)), dma((3, 2)), dma((3, 2)), dma((3, 2, 2)), dma((3, 2, 2)),
            dma((2, 3, 3)), dma((2, 3, 3)),
            *[dma((8,)) for _ in range(10)],
        ],
        compiler_params=pltpu.CompilerParams(
            collective_id=0, has_side_effects=True, vmem_limit_bytes=60 << 20
        ),
        cost_estimate=pl.CostEstimate(
            flops=2 * (atoms * size) ** 2 * points, bytes_accessed=20 << 20, transcendentals=0
        ),
    )(first, second, weights.reshape(-1, size), basis, density, inverse)


def local(
    basis_values,
    potential,
    pair_atoms,
    target_device,
    target_block,
    density,
    density_mask,
    inverse_intersection,
    inverse_mask,
):
    atoms, _, size = basis_values.shape
    tile_blocks = density_mask.shape[0]
    devices = lax.axis_size(ALL)
    per_owner = tile_blocks * tile_blocks // lax.axis_size("panel")
    empty = atoms * atoms

    target = target_device[:, 0] * per_owner + target_block
    serial = jnp.arange(target.shape[0], dtype=jnp.int32)
    key = serial * empty + pair_atoms[0] * atoms + pair_atoms[1]
    hit = target[None, :] == jnp.arange(devices * per_owner, dtype=jnp.int32)[:, None]
    low = jnp.min(jnp.where(hit, key[None, :], 1 << 30), axis=1)
    high = jnp.max(jnp.where(hit, key[None, :], -1), axis=1)
    first = jnp.where(high >= 0, low % empty, empty)
    second = jnp.where(high > low, high % empty, empty)

    density_used = masked_blocks(density, density_mask, size)
    inverse_used = masked_blocks(inverse_intersection, inverse_mask, size)
    width = inverse_used.shape[1] // lax.axis_size("panel")
    own = lax.dynamic_slice_in_dim(inverse_used, lax.axis_index("panel") * width, width, 1)
    return gradient_tile(first, second, potential, basis_values, density_used, own)


def solution(mesh):
    placed = (
        P(ALL, None, None),
        P(ALL),
        P(None, ALL),
        P(ALL, None),
        P(ALL),
        P("row", "col"),
        P("row", "col"),
        P("row", "col"),
        P("row", "col"),
    )
    return jax.shard_map(
        local, mesh=mesh, in_specs=placed, out_specs=P("row", ("col", "panel")), check_vma=False
    )
```

```python
import functools

import jax
import jax.numpy as jnp
from jax import lax
from jax.experimental import pallas as pl
from jax.experimental.pallas import tpu as pltpu
from jax.sharding import PartitionSpec as P

ALL = ("row", "col", "panel")


def masked_blocks(matrix, block_mask, block_size):
    mask_rows, mask_cols = block_mask.shape
    shaped = matrix.reshape(mask_rows, block_size, mask_cols, block_size)
    factor = block_mask.astype(matrix.dtype)[:, None, :, None]
    return (shaped * factor).reshape(mask_rows * block_size, mask_cols * block_size)


SIZE = 128
SHARES = (48, 48, 32)
STARTS = (0, 48, 96)
ORDERS = (("x", "y", "z"), ("z", "x", "y"), ("y", "z", "x"))


def place():
    row, col, core = (lax.axis_index(axis) for axis in ALL)
    return {"x": col % 2 * 2 + row % 2, "y": row // 2, "z": col // 2, "core": core}


def device_at(spot):
    return (spot["y"] * 2 + spot["x"] % 2, spot["z"] * 2 + spot["x"] // 2, spot["core"])


def moved(spot, axis, steps):
    return {**spot, axis: (spot[axis] + steps) % (2 if axis == "core" else 4)}


def tile_column(spot):
    return spot["z"] * 2 + spot["x"] // 2


def tile_row(spot):
    return spot["y"] * 2 + spot["x"] % 2


STEPS = ((2, 1), (1, 1), (3, 1), (2, 0), (0, 1), (1, 0), (3, 0))


class Gather:
    def __init__(self, here, ring, mirror, view, send, recv):
        self.here, self.ring, self.mirror, self.view, self.send, self.recv = here, ring, mirror, view, send, recv

    def spot(self, steps, image):
        there = moved(self.here, self.ring, steps)
        x = there["x"]
        if image and self.mirror == "x_hi":
            x = (x + 2) % 4
        elif image:
            x = x // 2 * 2 + (x + 1) % 2
        return {**there, "x": x}

    def copy(self, ref, at, spot):
        return pltpu.make_async_remote_copy(
            src_ref=ref, dst_ref=ref, send_sem=self.send.at[at], recv_sem=self.recv.at[at],
            device_id=device_at(spot), device_id_type=pl.DeviceIdType.MESH,
        )

    def cross(self):
        return self.copy(self.view(self.here, None), 0, self.spot(0, 1))

    def hop(self, side, image):
        ref = self.view(self.spot(0, image), None)
        return self.copy(ref, 1 + side * 2 + image, self.spot(3 if side else 1, 0))

    def far(self, side, image):
        ref = self.view(self.spot(1 if side else 3, image), side)
        return self.copy(ref, 5 + side * 2 + image, self.spot(3 if side else 1, 0))

    def begin(self):
        self.cross().start()
        self.hop(0, 0).start()
        self.hop(1, 0).start()

    def second(self):
        self.cross().wait_recv()
        for side in range(2):
            self.hop(side, 1).start()
        for side in range(2):
            self.hop(side, 0).wait_recv()
            self.far(side, 0).start()

    def third(self):
        for side in range(2):
            self.hop(side, 1).wait_recv()
            self.far(side, 1).start()

    def finish(self):
        for side in range(2):
            for image in range(2):
                self.far(side, image).wait_recv()

    def sent(self):
        self.cross().wait_send()
        for side in range(2):
            for image in range(2):
                self.hop(side, image).wait_send()
                self.far(side, image).wait_send()


def whole_kernel(
    first_ref, second_ref, weight_ref, basis_ref, density_ref, inverse_ref, out_ref,
    raw, left, right, blocks, column,
    own0, own1, own2, give0, give1, give2, pair0, pair1, pair2,
    relay0, relay1, relay2, near0, near1, near2, one0, one1, one2,
    got20, got21, got22, two0, two1, two2, got30, got31, got32,
    p_row, s_col, x_col, row_buf,
    fetch_sem, pair_send, pair_recv, relay_send, relay_recv, near_send, near_recv, send_sem, recv_sem,
    p_send, p_recv, s_send, s_recv, x_send, x_recv, gather_send, gather_recv, share_send, share_recv,
):
    here = place()
    own, give, pair = (own0, own1, own2), (give0, give1, give2), (pair0, pair1, pair2)
    relay, near, one = (relay0, relay1, relay2), (near0, near1, near2), (one0, one1, one2)
    two = (two0, two1, two2)
    sources, lands = (None, one, two), (None, (got20, got21, got22), (got30, got31, got32))
    partner = moved(here, "core", 1)
    mesh = pl.DeviceIdType.MESH
    atoms, points, size = basis_ref.shape
    chunks = points // size
    slots = raw.shape[0]

    def fetch(a):
        return pltpu.make_async_copy(basis_ref.at[a], raw.at[a % slots], fetch_sem.at[a])

    for a in range(slots):
        fetch(a).start()

    peers = [partner]
    for axis in ("x", "y", "z"):
        peers += [moved(here, axis, d) for d in (1, 2, 3)]
    peers += [moved(moved(here, "x", 2), "z", d) for d in (1, 2, 3)]
    barrier = pltpu.get_barrier_semaphore()
    for peer in peers:
        pl.semaphore_signal(barrier, inc=1, device_id=device_at(peer), device_id_type=mesh)

    for k in range(chunks):
        spread_row = jnp.broadcast_to(weight_ref[k : k + 1, :], (size, size))
        column[k * size : (k + 1) * size, :] = spread_row.T
    blocks[atoms * atoms] = jnp.zeros((size, size), jnp.bfloat16)

    def remote(src, dst, send, recv, spot):
        return pltpu.make_async_remote_copy(
            src_ref=src, dst_ref=dst, send_sem=send, recv_sem=recv,
            device_id=device_at(spot), device_id_type=mesh,
        )

    tile = 2 * size
    own_col = pl.ds(pl.multiple_of(tile_column(here) * tile, tile), tile)
    own_row = pl.ds(pl.multiple_of(tile_row(here) * tile, tile), tile)

    def p_view(spot, half):
        rows = pl.ds(0, tile) if half is None else pl.ds(half * size, size)
        return p_row.at[rows, pl.ds(pl.multiple_of(tile_column(spot) * tile, tile), tile)]

    def row_view(ref):
        def view(spot, half):
            start = tile_row(spot) * tile + (half or 0) * size
            return ref.at[pl.ds(pl.multiple_of(start, size), tile if half is None else size), :]

        return view

    p_all = Gather(here, "z", "x_hi", p_view, p_send, p_recv)
    s_all = Gather(here, "y", "x_lo", row_view(s_col), s_send, s_recv)
    x_all = Gather(here, "y", "x_lo", row_view(x_col), x_send, x_recv)

    p_row[:, own_col] = density_ref[...]
    s_col[own_row, :] = inverse_ref[...]
    pl.semaphore_wait(barrier, len(peers))
    p_all.begin()
    s_all.begin()

    def prepare(a):
        fetch(a).wait()
        cols = pl.ds(a * size, size)
        for k in range(chunks):
            rows = pl.ds(k * size, size)
            piece = raw[a % slots, rows, :]
            left[cols, rows] = piece.T
            scaled = piece.astype(jnp.float32) * column[rows, :]
            right[rows, cols] = scaled.astype(jnp.bfloat16)
        if a < atoms - slots:
            fetch(a + slots).start()

    for a in range(atoms):
        prepare(a)
    for j in range(0, atoms, 2):
        cols = pl.ds(j * size, tile)
        product = jnp.dot(left[: (j + 2) * size, :], right[:, cols], preferred_element_type=jnp.float32)
        for u in range(j + 2):
            for v in range(2):
                part = product[u * size : (u + 1) * size, v * size : (v + 1) * size].astype(jnp.bfloat16)
                blocks[u * atoms + j + v] = part
                if u < j:
                    blocks[(j + v) * atoms + u] = part.T
        if j == 4:
            p_all.second()
            s_all.second()
        if j == 10:
            p_all.third()
            s_all.third()

    def spot_of(k, d):
        return (here[ORDERS[k][0]] + d) % 4

    def assembled(k, q, m, g, core):
        at = dict(zip(ORDERS[k], (q, m, g // 2)))
        n = ((tile_row(at) * 8 + tile_column(at)) * 2 + core) * 2 + g % 2
        rows = pl.ds(STARTS[k], SHARES[k])
        return blocks[first_ref[n], rows, :] + blocks[second_ref[n], rows, :]

    def swap(k, d):
        q = spot_of(k, d)
        return remote(give[k].at[q], pair[k].at[q], pair_send.at[k, d], pair_recv.at[k, d], partner)

    def pass_relay(k, side):
        half = pl.ds(16 * side, 16)
        return remote(
            own[k].at[spot_of(k, 2), half], relay[k].at[side], relay_send.at[k, side], relay_recv.at[k, side],
            moved(here, ORDERS[k][0], 3 if side else 1),
        )

    def pass_near(k, side, part):
        half = pl.ds(16 * part, 16)
        d = 3 if side else 1
        return remote(
            own[k].at[spot_of(k, d), half], near[k].at[side, half],
            near_send.at[k, side, part], near_recv.at[k, side, part], moved(here, ORDERS[k][0], d),
        )

    def pass_on(stage, k, d):
        axis = ORDERS[k][stage]
        return remote(
            sources[stage][k].at[(here[axis] + d) % 4], lands[stage][k].at[d - 1],
            send_sem.at[stage - 1, k, d - 1], recv_sem.at[stage - 1, k, d - 1], moved(here, axis, d),
        )

    def give_away(d):
        for k in range(3):
            q = spot_of(k, d)

            @pl.loop(0, 4)
            def _(m):
                for g in range(8):
                    give[k][q, m * 8 + g] = assembled(k, q, m, g, partner["core"])

            swap(k, d).start()

    def take_in(d):
        for k in range(3):
            q = spot_of(k, d)
            swap(k, d).wait_recv()

            @pl.loop(0, 4)
            def _(m):
                for g in range(8):
                    own[k][q, m * 8 + g] = assembled(k, q, m, g, here["core"]) + pair[k][q, m * 8 + g]

            if d == 2:
                pass_relay(k, 0).start()
                pass_relay(k, 1).start()
            if d == 1:
                pass_near(k, 0, 1).start()
            if d == 3:
                pass_near(k, 1, 0).start()

    def pass_relayed(side):
        for k in range(3):
            q = spot_of(k, 3 if side else 1)
            pass_relay(k, side).wait_recv()

            @pl.loop(0, 4)
            def _(m):
                for g in range(4):
                    n = m * 4 + g
                    own[k][q, 16 * side + n] = own[k][q, 16 * side + n] + relay[k][side, n]

            pass_near(k, side, side).start()

    turns = (2, 1, 3, 0)
    give_away(2)
    give_away(1)
    take_in(2)
    give_away(3)
    take_in(1)
    give_away(0)
    p_all.finish()
    s_all.finish()
    x_col[own_row, :] = jnp.dot(p_row[...], s_col[...], preferred_element_type=jnp.float32).astype(jnp.bfloat16)
    take_in(3)
    pass_relayed(0)
    pass_relayed(1)
    take_in(0)
    for k in range(3):
        q = spot_of(k, 0)
        for side in range(2):
            for part in range(2):
                pass_near(k, side, part).wait_recv()

        @pl.loop(0, 4)
        def _(m):
            for g in range(8):
                n = m * 8 + g
                total = own[k][q, n].astype(jnp.float32) + near[k][0, n].astype(jnp.float32)
                one[k][m, g] = (total + near[k][1, n].astype(jnp.float32)).astype(jnp.bfloat16)

        for d in (2, 1, 3):
            pass_on(1, k, d).start()
    x_all.begin()

    def added(stage, k, n):
        mine = sources[stage][k][here[ORDERS[k][stage]], n].astype(jnp.float32)
        for d in range(3):
            mine = mine + lands[stage][k][d, n].astype(jnp.float32)
        return mine.astype(jnp.bfloat16)

    for k in range(3):
        for d in (1, 2, 3):
            pass_on(1, k, d).wait_recv()
        for q in range(4):
            for b in range(2):
                two[k][q, b] = added(1, k, q * 2 + b)
        for d in (2, 1, 3):
            pass_on(2, k, d).start()
    x_all.second()

    core_row = pl.multiple_of(here["core"] * size, size)
    for k in range(3):
        for d in (1, 2, 3):
            pass_on(2, k, d).wait_recv()
        for b in range(2):
            cols = pl.ds(pl.multiple_of(tile_column(here) * tile + b * size, size), size)
            row_buf[pl.ds(core_row + STARTS[k], SHARES[k]), cols] = added(2, k, b)

    def tile_of(steps, image):
        cols = pl.ds(pl.multiple_of(tile_column(p_all.spot(steps, image)) * tile, tile), tile)
        return row_buf.at[pl.ds(core_row, size), cols]

    def spread(steps, image):
        at = steps * 2 + image
        return remote(tile_of(0, 0), tile_of(0, 0), gather_send.at[at], gather_recv.at[at], p_all.spot(steps, image))

    def share(steps, image):
        ref = tile_of((4 - steps) % 4, image)
        at = steps * 2 + image
        return remote(ref, ref, share_send.at[at], share_recv.at[at], partner)

    for step in STEPS:
        spread(*step).start()
    share(0, 0).start()
    x_all.third()
    x_all.finish()
    for step in STEPS[::-1]:
        spread(*step).wait_recv()
        share(*step).start()
    for step in ((0, 0),) + STEPS:
        share(*step).wait_recv()
    out_ref[...] = jnp.dot(row_buf[...], x_col[...], preferred_element_type=jnp.float32)

    for gather in (p_all, s_all, x_all):
        gather.sent()
    for step in STEPS:
        spread(*step).wait_send()
        share(*step).wait_send()
    share(0, 0).wait_send()
    for k in range(3):
        for d in turns:
            swap(k, d).wait_send()
        for side in range(2):
            pass_relay(k, side).wait_send()
            for part in range(2):
                pass_near(k, side, part).wait_send()
        for stage in (1, 2):
            for d in (1, 2, 3):
                pass_on(stage, k, d).wait_send()


def gradient_tile(first, second, weights, basis, density, inverse):
    atoms, points, size = basis.shape
    depth = 16 * size

    def buffers(*lead):
        return [pltpu.VMEM((*lead, share, size), jnp.bfloat16) for share in SHARES]

    def plain(*shape):
        return pltpu.VMEM(shape, jnp.bfloat16)

    dma = pltpu.SemaphoreType.DMA
    vmem = pl.BlockSpec(memory_space=pltpu.VMEM)
    smem = pl.BlockSpec(memory_space=pltpu.SMEM)
    return pl.pallas_call(
        whole_kernel,
        out_shape=jax.ShapeDtypeStruct((2 * size, 2 * size), jnp.float32),
        in_specs=[smem, smem, vmem, pl.BlockSpec(memory_space=pl.ANY), vmem, vmem],
        out_specs=vmem,
        scratch_shapes=[
            plain(atoms // 2, points, size), plain(atoms * size, points), plain(points, atoms * size),
            plain(atoms * atoms + 1, size, size), pltpu.VMEM((points, size), jnp.float32),
            *buffers(4, 32), *buffers(4, 32), *buffers(4, 32),
            *buffers(2, 16), *buffers(2, 32), *buffers(4, 8),
            *buffers(3, 8), *buffers(4, 2), *buffers(3, 2),
            plain(2 * size, depth), plain(depth, 2 * size), plain(depth, 2 * size), plain(2 * size, depth),
            dma((atoms,)), dma((3, 4)), dma((3, 4)), dma((3, 2)), dma((3, 2)), dma((3, 2, 2)), dma((3, 2, 2)),
            dma((2, 3, 3)), dma((2, 3, 3)),
            *[dma((9,)) for _ in range(6)], *[dma((8,)) for _ in range(4)],
        ],
        compiler_params=pltpu.CompilerParams(
            collective_id=0, has_side_effects=True, vmem_limit_bytes=60 << 20
        ),
        cost_estimate=pl.CostEstimate(
            flops=2 * (atoms * size) ** 2 * points, bytes_accessed=20 << 20, transcendentals=0
        ),
    )(first, second, weights.reshape(-1, size), basis, density, inverse)


def local(
    basis_values,
    potential,
    pair_atoms,
    target_device,
    target_block,
    density,
    density_mask,
    inverse_intersection,
    inverse_mask,
):
    atoms, _, size = basis_values.shape
    tile_blocks = density_mask.shape[0]
    devices = lax.axis_size(ALL)
    per_owner = tile_blocks * tile_blocks // lax.axis_size("panel")
    empty = atoms * atoms

    target = target_device[:, 0] * per_owner + target_block
    serial = jnp.arange(target.shape[0], dtype=jnp.int32)
    key = serial * empty + pair_atoms[0] * atoms + pair_atoms[1]
    hit = target[None, :] == jnp.arange(devices * per_owner, dtype=jnp.int32)[:, None]
    low = jnp.min(jnp.where(hit, key[None, :], 1 << 30), axis=1)
    high = jnp.max(jnp.where(hit, key[None, :], -1), axis=1)
    first = jnp.where(high >= 0, low % empty, empty)
    second = jnp.where(high > low, high % empty, empty)

    density_used = masked_blocks(density, density_mask, size)
    inverse_used = masked_blocks(inverse_intersection, inverse_mask, size)
    width = inverse_used.shape[1] // lax.axis_size("panel")
    own = lax.dynamic_slice_in_dim(inverse_used, lax.axis_index("panel") * width, width, 1)
    return gradient_tile(first, second, potential, basis_values, density_used, own)


def solution(mesh):
    placed = (
        P(ALL, None, None),
        P(ALL),
        P(None, ALL),
        P(ALL, None),
        P(ALL),
        P("row", "col"),
        P("row", "col"),
        P("row", "col"),
        P("row", "col"),
    )
    return jax.shard_map(
        local, mesh=mesh, in_specs=placed, out_specs=P("row", ("col", "panel")), check_vma=False
    )
```

```python
import functools

import jax
import jax.numpy as jnp
from jax import lax
from jax.experimental import pallas as pl
from jax.experimental.pallas import tpu as pltpu
from jax.sharding import PartitionSpec as P

ALL = ("row", "col", "panel")


SIZE = 128
SHARES = (48, 48, 32)
STARTS = (0, 48, 96)
ORDERS = (("x", "y", "z"), ("z", "x", "y"), ("y", "z", "x"))


def place():
    row, col, core = (lax.axis_index(axis) for axis in ALL)
    return {"x": col % 2 * 2 + row % 2, "y": row // 2, "z": col // 2, "core": core}


def device_at(spot):
    return (spot["y"] * 2 + spot["x"] % 2, spot["z"] * 2 + spot["x"] // 2, spot["core"])


def moved(spot, axis, steps):
    return {**spot, axis: (spot[axis] + steps) % (2 if axis == "core" else 4)}


def tile_column(spot):
    return spot["z"] * 2 + spot["x"] // 2


def tile_row(spot):
    return spot["y"] * 2 + spot["x"] % 2


STEPS = ((2, 1), (1, 1), (3, 1), (2, 0), (0, 1), (1, 0), (3, 0))


class Gather:
    def __init__(self, here, ring, mirror, view, send, recv):
        self.here, self.ring, self.mirror, self.view, self.send, self.recv = here, ring, mirror, view, send, recv

    def spot(self, steps, image):
        there = moved(self.here, self.ring, steps)
        x = there["x"]
        if image and self.mirror == "x_hi":
            x = (x + 2) % 4
        elif image:
            x = x // 2 * 2 + (x + 1) % 2
        return {**there, "x": x}

    def copy(self, ref, at, spot):
        return pltpu.make_async_remote_copy(
            src_ref=ref, dst_ref=ref, send_sem=self.send.at[at], recv_sem=self.recv.at[at],
            device_id=device_at(spot), device_id_type=pl.DeviceIdType.MESH,
        )

    def cross(self):
        return self.copy(self.view(self.here, None), 0, self.spot(0, 1))

    def hop(self, side, image):
        ref = self.view(self.spot(0, image), None)
        return self.copy(ref, 1 + side * 2 + image, self.spot(3 if side else 1, 0))

    def far(self, side, image):
        ref = self.view(self.spot(1 if side else 3, image), side)
        return self.copy(ref, 5 + side * 2 + image, self.spot(3 if side else 1, 0))

    def begin(self):
        self.cross().start()
        self.hop(0, 0).start()
        self.hop(1, 0).start()

    def second(self):
        self.cross().wait_recv()
        for side in range(2):
            self.hop(side, 1).start()
        for side in range(2):
            self.hop(side, 0).wait_recv()
            self.far(side, 0).start()

    def third(self):
        for side in range(2):
            self.hop(side, 1).wait_recv()
            self.far(side, 1).start()

    def finish(self):
        for side in range(2):
            for image in range(2):
                self.far(side, image).wait_recv()

    def sent(self):
        self.cross().wait_send()
        for side in range(2):
            for image in range(2):
                self.hop(side, image).wait_send()
                self.far(side, image).wait_send()


def whole_kernel(
    owner_ref, block_ref, atoms_ref, weight_ref, basis_ref,
    density_ref, density_mask_ref, inverse_ref, inverse_mask_ref, out_ref,
    table, index_ref, inverse_half, raw, left, right, blocks, column,
    own0, own1, own2, give0, give1, give2, pair0, pair1, pair2,
    relay0, relay1, relay2, near0, near1, near2, one0, one1, one2,
    got20, got21, got22, two0, two1, two2, got30, got31, got32,
    p_row, s_col, x_col, row_buf,
    table_sem, half_sem, fetch_sem, pair_send, pair_recv, relay_send, relay_recv, near_send, near_recv, send_sem, recv_sem,
    p_send, p_recv, s_send, s_recv, x_send, x_recv, gather_send, gather_recv, share_send, share_recv,
):
    here = place()
    own, give, pair = (own0, own1, own2), (give0, give1, give2), (pair0, pair1, pair2)
    relay, near, one = (relay0, relay1, relay2), (near0, near1, near2), (one0, one1, one2)
    two = (two0, two1, two2)
    sources, lands = (None, one, two), (None, (got20, got21, got22), (got30, got31, got32))
    partner = moved(here, "core", 1)
    mesh = pl.DeviceIdType.MESH
    atoms, points, size = basis_ref.shape
    chunks = points // size
    slots = raw.shape[0]

    def fetch(a):
        return pltpu.make_async_copy(basis_ref.at[a], raw.at[a % slots], fetch_sem.at[a])

    tile = 2 * size
    half_cols = pl.ds(pl.multiple_of(here["core"] * tile, tile), tile)
    fetch_half = pltpu.make_async_copy(inverse_ref.at[:, half_cols], inverse_half, half_sem)
    fetch_half.start()
    for a in range(slots):
        fetch(a).start()

    peers = [partner]
    for axis in ("x", "y", "z"):
        peers += [moved(here, axis, d) for d in (1, 2, 3)]
    peers += [moved(moved(here, "x", 2), "z", d) for d in (1, 2, 3)]
    barrier = pltpu.get_barrier_semaphore()
    for peer in peers:
        pl.semaphore_signal(barrier, inc=1, device_id=device_at(peer), device_id_type=mesh)

    for k in range(chunks):
        spread_row = jnp.broadcast_to(weight_ref[k : k + 1, :], (size, size))
        column[k * size : (k + 1) * size, :] = spread_row.T

    def upright(row):
        return jnp.broadcast_to(row, (size, size)).T

    count = owner_ref.shape[1]
    serial = lax.broadcasted_iota(jnp.int32, (1, count), 1)
    target = upright(owner_ref[...] * 2 + block_ref[...])
    key = upright((serial * atoms + atoms_ref[0:1, :]) * atoms + atoms_ref[1:2, :])
    lane = lax.broadcasted_iota(jnp.int32, (size, size), 1)
    for part in range(table.shape[1] // size):
        hit = target == lane + part * size
        low = jnp.min(jnp.where(hit, key, 1 << 30), axis=0, keepdims=True)
        high = jnp.max(jnp.where(hit, key, -1), axis=0, keepdims=True)
        cols = pl.ds(part * size, size)
        table[0:1, cols] = jnp.where(high >= 0, low % (atoms * atoms), atoms * atoms)
        table[1:2, cols] = jnp.where(high > low, high % (atoms * atoms), atoms * atoms)
    fetch_table = pltpu.make_async_copy(table, index_ref, table_sem)
    fetch_table.start()
    blocks[atoms * atoms] = jnp.zeros((size, size), jnp.bfloat16)

    def remote(src, dst, send, recv, spot):
        return pltpu.make_async_remote_copy(
            src_ref=src, dst_ref=dst, send_sem=send, recv_sem=recv,
            device_id=device_at(spot), device_id_type=mesh,
        )

    own_col = pl.ds(pl.multiple_of(tile_column(here) * tile, tile), tile)
    own_row = pl.ds(pl.multiple_of(tile_row(here) * tile, tile), tile)

    def p_view(spot, half):
        rows = pl.ds(0, tile) if half is None else pl.ds(half * size, size)
        return p_row.at[rows, pl.ds(pl.multiple_of(tile_column(spot) * tile, tile), tile)]

    def row_view(ref):
        def view(spot, half):
            start = tile_row(spot) * tile + (half or 0) * size
            return ref.at[pl.ds(pl.multiple_of(start, size), tile if half is None else size), :]

        return view

    p_all = Gather(here, "z", "x_hi", p_view, p_send, p_recv)
    s_all = Gather(here, "y", "x_lo", row_view(s_col), s_send, s_recv)
    x_all = Gather(here, "y", "x_lo", row_view(x_col), x_send, x_recv)

    def masked(block, keep):
        return (block.astype(jnp.float32) * keep.astype(jnp.float32)).astype(jnp.bfloat16)

    fetch_half.wait()
    for i in range(2):
        for j in range(2):
            rows, cols = pl.ds(i * size, size), pl.ds(j * size, size)
            own_rows = pl.ds(pl.multiple_of(tile_row(here) * tile + i * size, size), size)
            own_cols = pl.ds(pl.multiple_of(tile_column(here) * tile + j * size, size), size)
            p_row[rows, own_cols] = masked(density_ref[rows, cols], density_mask_ref[i, j])
            s_col[own_rows, cols] = masked(inverse_half[rows, cols], inverse_mask_ref[i, here["core"] * 2 + j])
    pl.semaphore_wait(barrier, len(peers))
    p_all.begin()
    s_all.begin()

    def prepare(a):
        fetch(a).wait()
        cols = pl.ds(a * size, size)
        for k in range(chunks):
            rows = pl.ds(k * size, size)
            piece = raw[a % slots, rows, :]
            left[cols, rows] = piece.T
            scaled = piece.astype(jnp.float32) * column[rows, :]
            right[rows, cols] = scaled.astype(jnp.bfloat16)
        if a < atoms - slots:
            fetch(a + slots).start()

    for a in range(atoms):
        prepare(a)
    for j in range(0, atoms, 2):
        cols = pl.ds(j * size, tile)
        product = jnp.dot(left[: (j + 2) * size, :], right[:, cols], preferred_element_type=jnp.float32)
        for u in range(j + 2):
            for v in range(2):
                part = product[u * size : (u + 1) * size, v * size : (v + 1) * size].astype(jnp.bfloat16)
                blocks[u * atoms + j + v] = part
                if u < j:
                    blocks[(j + v) * atoms + u] = part.T
        if j == 4:
            p_all.second()
            s_all.second()
        if j == 10:
            p_all.third()
            s_all.third()

    def spot_of(k, d):
        return (here[ORDERS[k][0]] + d) % 4

    def assembled(k, q, m, g, core, also=None):
        at = dict(zip(ORDERS[k], (q, m, g // 2)))
        n = ((tile_row(at) * 8 + tile_column(at)) * 2 + core) * 2 + g % 2
        rows = pl.ds(STARTS[k], SHARES[k])
        if also is None:
            return blocks[index_ref[0, n], rows, :] + blocks[index_ref[1, n], rows, :]
        total = blocks[index_ref[0, n], rows, :].astype(jnp.float32) + blocks[index_ref[1, n], rows, :].astype(jnp.float32)
        return (total + also.astype(jnp.float32)).astype(jnp.bfloat16)

    def swap(k, d):
        q = spot_of(k, d)
        return remote(give[k].at[q], pair[k].at[q], pair_send.at[k, d], pair_recv.at[k, d], partner)

    def pass_relay(k, side):
        half = pl.ds(16 * side, 16)
        return remote(
            own[k].at[spot_of(k, 2), half], relay[k].at[side], relay_send.at[k, side], relay_recv.at[k, side],
            moved(here, ORDERS[k][0], 3 if side else 1),
        )

    def pass_near(k, side, part):
        half = pl.ds(16 * part, 16)
        d = 3 if side else 1
        return remote(
            own[k].at[spot_of(k, d), half], near[k].at[side, half],
            near_send.at[k, side, part], near_recv.at[k, side, part], moved(here, ORDERS[k][0], d),
        )

    def pass_on(stage, k, d):
        axis = ORDERS[k][stage]
        return remote(
            sources[stage][k].at[(here[axis] + d) % 4], lands[stage][k].at[d - 1],
            send_sem.at[stage - 1, k, d - 1], recv_sem.at[stage - 1, k, d - 1], moved(here, axis, d),
        )

    def give_away(d):
        for k in range(3):
            q = spot_of(k, d)

            @pl.loop(0, 4)
            def _(m):
                for g in range(8):
                    give[k][q, m * 8 + g] = assembled(k, q, m, g, partner["core"])

            swap(k, d).start()

    def take_in(d):
        for k in range(3):
            q = spot_of(k, d)
            swap(k, d).wait_recv()

            @pl.loop(0, 4)
            def _(m):
                for g in range(8):
                    own[k][q, m * 8 + g] = assembled(k, q, m, g, here["core"], pair[k][q, m * 8 + g])

            if d == 2:
                pass_relay(k, 0).start()
                pass_relay(k, 1).start()
            if d == 1:
                pass_near(k, 0, 1).start()
            if d == 3:
                pass_near(k, 1, 0).start()

    def pass_relayed(side):
        for k in range(3):
            q = spot_of(k, 3 if side else 1)
            pass_relay(k, side).wait_recv()

            @pl.loop(0, 4)
            def _(m):
                for g in range(4):
                    n = m * 4 + g
                    own[k][q, 16 * side + n] = own[k][q, 16 * side + n] + relay[k][side, n]

            pass_near(k, side, side).start()

    turns = (2, 1, 3, 0)
    fetch_table.wait()
    give_away(2)
    give_away(1)
    take_in(2)
    give_away(3)
    take_in(1)
    give_away(0)
    p_all.finish()
    s_all.finish()
    x_col[own_row, :] = jnp.dot(p_row[...], s_col[...], preferred_element_type=jnp.float32).astype(jnp.bfloat16)
    take_in(3)
    pass_relayed(0)
    pass_relayed(1)
    take_in(0)
    for k in range(3):
        q = spot_of(k, 0)
        for side in range(2):
            for part in range(2):
                pass_near(k, side, part).wait_recv()

        @pl.loop(0, 4)
        def _(m):
            for g in range(8):
                n = m * 8 + g
                total = own[k][q, n].astype(jnp.float32) + near[k][0, n].astype(jnp.float32)
                one[k][m, g] = (total + near[k][1, n].astype(jnp.float32)).astype(jnp.bfloat16)

        for d in (2, 1, 3):
            pass_on(1, k, d).start()
    x_all.begin()

    def added(stage, k, n):
        mine = sources[stage][k][here[ORDERS[k][stage]], n].astype(jnp.float32)
        for d in range(3):
            mine = mine + lands[stage][k][d, n].astype(jnp.float32)
        return mine.astype(jnp.bfloat16)

    for k in range(3):
        for d in (1, 2, 3):
            pass_on(1, k, d).wait_recv()
        for q in range(4):
            for b in range(2):
                two[k][q, b] = added(1, k, q * 2 + b)
        for d in (2, 1, 3):
            pass_on(2, k, d).start()
    x_all.second()

    core_row = pl.multiple_of(here["core"] * size, size)
    for k in range(3):
        for d in (1, 2, 3):
            pass_on(2, k, d).wait_recv()
        for b in range(2):
            cols = pl.ds(pl.multiple_of(tile_column(here) * tile + b * size, size), size)
            row_buf[pl.ds(core_row + STARTS[k], SHARES[k]), cols] = added(2, k, b)

    def tile_of(steps, image):
        cols = pl.ds(pl.multiple_of(tile_column(p_all.spot(steps, image)) * tile, tile), tile)
        return row_buf.at[pl.ds(core_row, size), cols]

    def spread(steps, image):
        at = steps * 2 + image
        return remote(tile_of(0, 0), tile_of(0, 0), gather_send.at[at], gather_recv.at[at], p_all.spot(steps, image))

    def share(steps, image):
        ref = tile_of((4 - steps) % 4, image)
        at = steps * 2 + image
        return remote(ref, ref, share_send.at[at], share_recv.at[at], partner)

    for step in STEPS:
        spread(*step).start()
    share(0, 0).start()
    x_all.third()
    x_all.finish()
    for step in STEPS[::-1]:
        spread(*step).wait_recv()
        share(*step).start()
    for step in ((0, 0),) + STEPS:
        share(*step).wait_recv()
    out_ref[...] = jnp.dot(row_buf[...], x_col[...], preferred_element_type=jnp.float32)

    for gather in (p_all, s_all, x_all):
        gather.sent()
    for step in STEPS:
        spread(*step).wait_send()
        share(*step).wait_send()
    share(0, 0).wait_send()
    for k in range(3):
        for d in turns:
            swap(k, d).wait_send()
        for side in range(2):
            pass_relay(k, side).wait_send()
            for part in range(2):
                pass_near(k, side, part).wait_send()
        for stage in (1, 2):
            for d in (1, 2, 3):
                pass_on(stage, k, d).wait_send()


def gradient_tile(owner, block, pairs, weights, basis, density, density_mask, inverse, inverse_mask):
    atoms, points, size = basis.shape
    depth = 16 * size

    def buffers(*lead):
        return [pltpu.VMEM((*lead, share, size), jnp.bfloat16) for share in SHARES]

    def plain(*shape):
        return pltpu.VMEM(shape, jnp.bfloat16)

    dma = pltpu.SemaphoreType.DMA
    vmem = pl.BlockSpec(memory_space=pltpu.VMEM)
    smem = pl.BlockSpec(memory_space=pltpu.SMEM)
    hbm = pl.BlockSpec(memory_space=pl.ANY)
    return pl.pallas_call(
        whole_kernel,
        out_shape=jax.ShapeDtypeStruct((2 * size, 2 * size), jnp.float32),
        in_specs=[vmem, vmem, vmem, vmem, hbm, vmem, smem, hbm, smem],
        out_specs=vmem,
        scratch_shapes=[
            pltpu.VMEM((2, 2 * size), jnp.int32), pltpu.SMEM((2, 2 * size), jnp.int32), plain(2 * size, 2 * size),
            plain(atoms // 2, points, size), plain(atoms * size, points), plain(points, atoms * size),
            plain(atoms * atoms + 1, size, size), pltpu.VMEM((points, size), jnp.float32),
            *buffers(4, 32), *buffers(4, 32), *buffers(4, 32),
            *buffers(2, 16), *buffers(2, 32), *buffers(4, 8),
            *buffers(3, 8), *buffers(4, 2), *buffers(3, 2),
            plain(2 * size, depth), plain(depth, 2 * size), plain(depth, 2 * size), plain(2 * size, depth),
            dma, dma, dma((atoms,)), dma((3, 4)), dma((3, 4)), dma((3, 2)), dma((3, 2)), dma((3, 2, 2)), dma((3, 2, 2)),
            dma((2, 3, 3)), dma((2, 3, 3)),
            *[dma((9,)) for _ in range(6)], *[dma((8,)) for _ in range(4)],
        ],
        compiler_params=pltpu.CompilerParams(
            collective_id=0, has_side_effects=True, vmem_limit_bytes=60 << 20
        ),
        cost_estimate=pl.CostEstimate(
            flops=2 * (atoms * size) ** 2 * points, bytes_accessed=20 << 20, transcendentals=0
        ),
    )(
        owner.reshape(1, -1), block.reshape(1, -1), pairs, weights.reshape(-1, size), basis,
        density, density_mask, inverse, inverse_mask,
    )


def local(
    basis_values,
    potential,
    pair_atoms,
    target_device,
    target_block,
    density,
    density_mask,
    inverse_intersection,
    inverse_mask,
):
    return gradient_tile(
        target_device,
        target_block,
        pair_atoms,
        potential,
        basis_values,
        density,
        density_mask,
        inverse_intersection,
        inverse_mask,
    )


def solution(mesh):
    placed = (
        P(ALL, None, None),
        P(ALL),
        P(None, ALL),
        P(ALL, None),
        P(ALL),
        P("row", "col"),
        P("row", "col"),
        P("row", "col"),
        P("row", "col"),
    )
    return jax.shard_map(
        local, mesh=mesh, in_specs=placed, out_specs=P("row", ("col", "panel")), check_vma=False
    )
```

```python
import functools

import jax
import jax.numpy as jnp
from jax import lax
from jax.experimental import pallas as pl
from jax.experimental.pallas import tpu as pltpu
from jax.sharding import PartitionSpec as P

ALL = ("row", "col", "panel")


SIZE = 128
SHARES = (48, 48, 32)
STARTS = (0, 48, 96)
ORDERS = (("x", "y", "z"), ("z", "x", "y"), ("y", "z", "x"))


def place():
    row, col, core = (lax.axis_index(axis) for axis in ALL)
    return {"x": col % 2 * 2 + row % 2, "y": row // 2, "z": col // 2, "core": core}


def device_at(spot):
    return (spot["y"] * 2 + spot["x"] % 2, spot["z"] * 2 + spot["x"] // 2, spot["core"])


def moved(spot, axis, steps):
    return {**spot, axis: (spot[axis] + steps) % (2 if axis == "core" else 4)}


def tile_column(spot):
    return spot["z"] * 2 + spot["x"] // 2


def tile_row(spot):
    return spot["y"] * 2 + spot["x"] % 2


STEPS = ((2, 1), (1, 1), (3, 1), (2, 0), (0, 1), (1, 0), (3, 0))


class Gather:
    def __init__(self, here, ring, mirror, view, send, recv):
        self.here, self.ring, self.mirror, self.view, self.send, self.recv = here, ring, mirror, view, send, recv

    def spot(self, steps, image):
        there = moved(self.here, self.ring, steps)
        x = there["x"]
        if image and self.mirror == "x_hi":
            x = (x + 2) % 4
        elif image:
            x = x // 2 * 2 + (x + 1) % 2
        return {**there, "x": x}

    def copy(self, ref, at, spot):
        return pltpu.make_async_remote_copy(
            src_ref=ref, dst_ref=ref, send_sem=self.send.at[at], recv_sem=self.recv.at[at],
            device_id=device_at(spot), device_id_type=pl.DeviceIdType.MESH,
        )

    def cross(self):
        return self.copy(self.view(self.here, None), 0, self.spot(0, 1))

    def hop(self, side, image):
        ref = self.view(self.spot(0, image), None)
        return self.copy(ref, 1 + side * 2 + image, self.spot(3 if side else 1, 0))

    def far(self, side, image):
        ref = self.view(self.spot(1 if side else 3, image), side)
        return self.copy(ref, 5 + side * 2 + image, self.spot(3 if side else 1, 0))

    def begin(self):
        self.cross().start()
        self.hop(0, 0).start()
        self.hop(1, 0).start()

    def second(self):
        self.cross().wait_recv()
        for side in range(2):
            self.hop(side, 1).start()
        for side in range(2):
            self.hop(side, 0).wait_recv()
            self.far(side, 0).start()

    def third(self):
        for side in range(2):
            self.hop(side, 1).wait_recv()
            self.far(side, 1).start()

    def finish(self):
        for side in range(2):
            for image in range(2):
                self.far(side, image).wait_recv()

    def sent(self):
        self.cross().wait_send()
        for side in range(2):
            for image in range(2):
                self.hop(side, image).wait_send()
                self.far(side, image).wait_send()


def whole_kernel(
    owner_in, block_in, atoms_in, weight_in, basis_ref, density_in, density_mask_in, inverse_ref, inverse_mask_in, out_ref,
    owner_ref, block_ref, atoms_ref, weight_ref, density_ref, density_mask_ref, inverse_mask_ref, small_sem,
    table, index_ref, inverse_half, raw, left, right, blocks, column,
    own0, own1, own2, give0, give1, give2, pair0, pair1, pair2,
    relay0, relay1, relay2, near0, near1, near2, one0, one1, one2,
    got20, got21, got22, two0, two1, two2, got30, got31, got32,
    p_row, s_col, x_col, row_buf,
    table_sem, half_sem, fetch_sem, pair_send, pair_recv, relay_send, relay_recv, near_send, near_recv, send_sem, recv_sem,
    p_send, p_recv, s_send, s_recv, x_send, x_recv, gather_send, gather_recv, share_send, share_recv,
):
    here = place()
    own, give, pair = (own0, own1, own2), (give0, give1, give2), (pair0, pair1, pair2)
    relay, near, one = (relay0, relay1, relay2), (near0, near1, near2), (one0, one1, one2)
    two = (two0, two1, two2)
    sources, lands = (None, one, two), (None, (got20, got21, got22), (got30, got31, got32))
    partner = moved(here, "core", 1)
    mesh = pl.DeviceIdType.MESH
    atoms, points, size = basis_ref.shape
    chunks = points // size
    slots = raw.shape[0]

    def fetch(a):
        return pltpu.make_async_copy(basis_ref.at[a], raw.at[a % slots], fetch_sem.at[a])

    peers = [partner]
    for axis in ("x", "y", "z"):
        peers += [moved(here, axis, d) for d in (1, 2, 3)]
    peers += [moved(moved(here, "x", 2), "z", d) for d in (1, 2, 3)]
    barrier = pltpu.get_barrier_semaphore()
    for peer in peers:
        pl.semaphore_signal(barrier, inc=1, device_id=device_at(peer), device_id_type=mesh)

    tile = 2 * size
    half_cols = pl.ds(pl.multiple_of(here["core"] * tile, tile), tile)
    fetch_half = pltpu.make_async_copy(inverse_ref.at[:, half_cols], inverse_half, half_sem)
    fetch_half.start()
    small = [
        pltpu.make_async_copy(source, held, small_sem.at[i])
        for i, (source, held) in enumerate(
            (
                (weight_in, weight_ref), (owner_in, owner_ref), (block_in, block_ref), (atoms_in, atoms_ref),
                (density_in, density_ref), (density_mask_in, density_mask_ref), (inverse_mask_in, inverse_mask_ref),
            )
        )
    ]
    for copy in small:
        copy.start()
    for a in range(slots):
        fetch(a).start()

    for copy in small:
        copy.wait()
    for k in range(chunks):
        spread_row = jnp.broadcast_to(weight_ref[k : k + 1, :], (size, size))
        column[k * size : (k + 1) * size, :] = spread_row.T

    def upright(row):
        return jnp.broadcast_to(row, (size, size)).T

    count = owner_ref.shape[1]
    serial = lax.broadcasted_iota(jnp.int32, (1, count), 1)
    target = upright(owner_ref[...] * 2 + block_ref[...])
    key = upright((serial * atoms + atoms_ref[0:1, :]) * atoms + atoms_ref[1:2, :])
    lane = lax.broadcasted_iota(jnp.int32, (size, size), 1)
    for part in range(table.shape[1] // size):
        hit = target == lane + part * size
        low = jnp.min(jnp.where(hit, key, 1 << 30), axis=0, keepdims=True)
        high = jnp.max(jnp.where(hit, key, -1), axis=0, keepdims=True)
        cols = pl.ds(part * size, size)
        table[0:1, cols] = jnp.where(high >= 0, low % (atoms * atoms), atoms * atoms)
        table[1:2, cols] = jnp.where(high > low, high % (atoms * atoms), atoms * atoms)
    fetch_table = pltpu.make_async_copy(table, index_ref, table_sem)
    fetch_table.start()
    blocks[atoms * atoms] = jnp.zeros((size, size), jnp.bfloat16)

    def remote(src, dst, send, recv, spot):
        return pltpu.make_async_remote_copy(
            src_ref=src, dst_ref=dst, send_sem=send, recv_sem=recv,
            device_id=device_at(spot), device_id_type=mesh,
        )

    own_col = pl.ds(pl.multiple_of(tile_column(here) * tile, tile), tile)
    own_row = pl.ds(pl.multiple_of(tile_row(here) * tile, tile), tile)

    def p_view(spot, half):
        rows = pl.ds(0, tile) if half is None else pl.ds(half * size, size)
        return p_row.at[rows, pl.ds(pl.multiple_of(tile_column(spot) * tile, tile), tile)]

    def row_view(ref):
        def view(spot, half):
            start = tile_row(spot) * tile + (half or 0) * size
            return ref.at[pl.ds(pl.multiple_of(start, size), tile if half is None else size), :]

        return view

    p_all = Gather(here, "z", "x_hi", p_view, p_send, p_recv)
    s_all = Gather(here, "y", "x_lo", row_view(s_col), s_send, s_recv)
    x_all = Gather(here, "y", "x_lo", row_view(x_col), x_send, x_recv)

    def masked(block, keep):
        return (block.astype(jnp.float32) * keep.astype(jnp.float32)).astype(jnp.bfloat16)

    fetch_half.wait()
    for i in range(2):
        for j in range(2):
            rows, cols = pl.ds(i * size, size), pl.ds(j * size, size)
            own_rows = pl.ds(pl.multiple_of(tile_row(here) * tile + i * size, size), size)
            own_cols = pl.ds(pl.multiple_of(tile_column(here) * tile + j * size, size), size)
            p_row[rows, own_cols] = masked(density_ref[rows, cols], density_mask_ref[i, j])
            s_col[own_rows, cols] = masked(inverse_half[rows, cols], inverse_mask_ref[i, here["core"] * 2 + j])
    pl.semaphore_wait(barrier, len(peers))
    p_all.begin()
    s_all.begin()

    def prepare(a):
        fetch(a).wait()
        cols = pl.ds(a * size, size)
        for k in range(chunks):
            rows = pl.ds(k * size, size)
            piece = raw[a % slots, rows, :]
            left[cols, rows] = piece.T
            scaled = piece.astype(jnp.float32) * column[rows, :]
            right[rows, cols] = scaled.astype(jnp.bfloat16)
        if a < atoms - slots:
            fetch(a + slots).start()

    for a in range(atoms):
        prepare(a)
    for j in range(0, atoms, 2):
        cols = pl.ds(j * size, tile)
        product = jnp.dot(left[: (j + 2) * size, :], right[:, cols], preferred_element_type=jnp.float32)
        for u in range(j + 2):
            for v in range(2):
                part = product[u * size : (u + 1) * size, v * size : (v + 1) * size].astype(jnp.bfloat16)
                blocks[u * atoms + j + v] = part
                if u < j:
                    blocks[(j + v) * atoms + u] = part.T
        if j == 4:
            p_all.second()
            s_all.second()
        if j == 10:
            p_all.third()
            s_all.third()

    def spot_of(k, d):
        return (here[ORDERS[k][0]] + d) % 4

    def assembled(k, q, m, g, core, also=None):
        at = dict(zip(ORDERS[k], (q, m, g // 2)))
        n = ((tile_row(at) * 8 + tile_column(at)) * 2 + core) * 2 + g % 2
        rows = pl.ds(STARTS[k], SHARES[k])
        if also is None:
            return blocks[index_ref[0, n], rows, :] + blocks[index_ref[1, n], rows, :]
        total = blocks[index_ref[0, n], rows, :].astype(jnp.float32) + blocks[index_ref[1, n], rows, :].astype(jnp.float32)
        return (total + also.astype(jnp.float32)).astype(jnp.bfloat16)

    def swap(k, d):
        q = spot_of(k, d)
        return remote(give[k].at[q], pair[k].at[q], pair_send.at[k, d], pair_recv.at[k, d], partner)

    def pass_relay(k, side):
        half = pl.ds(16 * side, 16)
        return remote(
            own[k].at[spot_of(k, 2), half], relay[k].at[side], relay_send.at[k, side], relay_recv.at[k, side],
            moved(here, ORDERS[k][0], 3 if side else 1),
        )

    def pass_near(k, side, part):
        half = pl.ds(16 * part, 16)
        d = 3 if side else 1
        return remote(
            own[k].at[spot_of(k, d), half], near[k].at[side, half],
            near_send.at[k, side, part], near_recv.at[k, side, part], moved(here, ORDERS[k][0], d),
        )

    def pass_on(stage, k, d):
        axis = ORDERS[k][stage]
        return remote(
            sources[stage][k].at[(here[axis] + d) % 4], lands[stage][k].at[d - 1],
            send_sem.at[stage - 1, k, d - 1], recv_sem.at[stage - 1, k, d - 1], moved(here, axis, d),
        )

    def give_away(d):
        for k in range(3):
            q = spot_of(k, d)

            @pl.loop(0, 4)
            def _(m):
                for g in range(8):
                    give[k][q, m * 8 + g] = assembled(k, q, m, g, partner["core"])

            swap(k, d).start()

    def take_in(d):
        for k in range(3):
            q = spot_of(k, d)
            swap(k, d).wait_recv()

            @pl.loop(0, 4)
            def _(m):
                for g in range(8):
                    own[k][q, m * 8 + g] = assembled(k, q, m, g, here["core"], pair[k][q, m * 8 + g])

            if d == 2:
                pass_relay(k, 0).start()
                pass_relay(k, 1).start()
            if d == 1:
                pass_near(k, 0, 1).start()
            if d == 3:
                pass_near(k, 1, 0).start()

    def pass_relayed(side):
        for k in range(3):
            q = spot_of(k, 3 if side else 1)
            pass_relay(k, side).wait_recv()

            @pl.loop(0, 4)
            def _(m):
                for g in range(4):
                    n = m * 4 + g
                    own[k][q, 16 * side + n] = own[k][q, 16 * side + n] + relay[k][side, n]

            pass_near(k, side, side).start()

    turns = (2, 1, 3, 0)
    fetch_table.wait()
    give_away(2)
    give_away(1)
    take_in(2)
    give_away(3)
    take_in(1)
    give_away(0)
    p_all.finish()
    s_all.finish()
    x_col[own_row, :] = jnp.dot(p_row[...], s_col[...], preferred_element_type=jnp.float32).astype(jnp.bfloat16)
    take_in(3)
    pass_relayed(0)
    pass_relayed(1)
    take_in(0)
    x_all.begin()
    for k in range(3):
        q = spot_of(k, 0)
        for side in range(2):
            for part in range(2):
                pass_near(k, side, part).wait_recv()

        for d in turns:
            m = (here[ORDERS[k][1]] + d) % 4
            for g in range(8):
                n = m * 8 + g
                total = own[k][q, n].astype(jnp.float32) + near[k][0, n].astype(jnp.float32)
                one[k][m, g] = (total + near[k][1, n].astype(jnp.float32)).astype(jnp.bfloat16)
            if d:
                pass_on(1, k, d).start()

    def added(stage, k, n):
        mine = sources[stage][k][here[ORDERS[k][stage]], n].astype(jnp.float32)
        for d in range(3):
            mine = mine + lands[stage][k][d, n].astype(jnp.float32)
        return mine.astype(jnp.bfloat16)

    for k in range(3):
        for d in (1, 2, 3):
            pass_on(1, k, d).wait_recv()
        for d in turns:
            q = (here[ORDERS[k][2]] + d) % 4
            for b in range(2):
                two[k][q, b] = added(1, k, q * 2 + b)
            if d:
                pass_on(2, k, d).start()
    x_all.second()

    core_row = pl.multiple_of(here["core"] * size, size)
    for k in range(3):
        for d in (1, 2, 3):
            pass_on(2, k, d).wait_recv()
        for b in range(2):
            cols = pl.ds(pl.multiple_of(tile_column(here) * tile + b * size, size), size)
            row_buf[pl.ds(core_row + STARTS[k], SHARES[k]), cols] = added(2, k, b)

    def tile_of(steps, image):
        cols = pl.ds(pl.multiple_of(tile_column(p_all.spot(steps, image)) * tile, tile), tile)
        return row_buf.at[pl.ds(core_row, size), cols]

    def spread(steps, image):
        at = steps * 2 + image
        return remote(tile_of(0, 0), tile_of(0, 0), gather_send.at[at], gather_recv.at[at], p_all.spot(steps, image))

    def share(steps, image):
        ref = tile_of((4 - steps) % 4, image)
        at = steps * 2 + image
        return remote(ref, ref, share_send.at[at], share_recv.at[at], partner)

    for step in STEPS:
        spread(*step).start()
    share(0, 0).start()
    x_all.third()
    x_all.finish()
    for step in STEPS[::-1]:
        spread(*step).wait_recv()
        share(*step).start()
    def finish_rows(start):
        rows = pl.ds(pl.multiple_of(start, size), size)
        out_ref[rows, :] = jnp.dot(row_buf[rows, :], x_col[...], preferred_element_type=jnp.float32)

    finish_rows(core_row)
    for step in ((0, 0),) + STEPS:
        share(*step).wait_recv()
    finish_rows(size - core_row)

    for gather in (p_all, s_all, x_all):
        gather.sent()
    for step in STEPS:
        spread(*step).wait_send()
        share(*step).wait_send()
    share(0, 0).wait_send()
    for k in range(3):
        for d in turns:
            swap(k, d).wait_send()
        for side in range(2):
            pass_relay(k, side).wait_send()
            for part in range(2):
                pass_near(k, side, part).wait_send()
        for stage in (1, 2):
            for d in (1, 2, 3):
                pass_on(stage, k, d).wait_send()


def gradient_tile(owner, block, pairs, weights, basis, density, density_mask, inverse, inverse_mask):
    atoms, points, size = basis.shape
    depth = 16 * size

    def buffers(*lead):
        return [pltpu.VMEM((*lead, share, size), jnp.bfloat16) for share in SHARES]

    def plain(*shape):
        return pltpu.VMEM(shape, jnp.bfloat16)

    dma = pltpu.SemaphoreType.DMA
    vmem = pl.BlockSpec(memory_space=pltpu.VMEM)
    hbm = pl.BlockSpec(memory_space=pl.ANY)
    return pl.pallas_call(
        whole_kernel,
        out_shape=jax.ShapeDtypeStruct((2 * size, 2 * size), jnp.float32),
        in_specs=[hbm] * 9,
        out_specs=vmem,
        scratch_shapes=[
            pltpu.VMEM((1, owner.shape[0]), jnp.int32), pltpu.VMEM((1, owner.shape[0]), jnp.int32),
            pltpu.VMEM(pairs.shape, jnp.int32), pltpu.VMEM((points // size, size), jnp.float32),
            plain(*density.shape), pltpu.SMEM(density_mask.shape, jnp.int32), pltpu.SMEM(inverse_mask.shape, jnp.int32),
            dma((7,)),
            pltpu.VMEM((2, 2 * size), jnp.int32), pltpu.SMEM((2, 2 * size), jnp.int32), plain(2 * size, 2 * size),
            plain(atoms // 2, points, size), plain(atoms * size, points), plain(points, atoms * size),
            plain(atoms * atoms + 1, size, size), pltpu.VMEM((points, size), jnp.float32),
            *buffers(4, 32), *buffers(4, 32), *buffers(4, 32),
            *buffers(2, 16), *buffers(2, 32), *buffers(4, 8),
            *buffers(3, 8), *buffers(4, 2), *buffers(3, 2),
            plain(2 * size, depth), plain(depth, 2 * size), plain(depth, 2 * size), plain(2 * size, depth),
            dma, dma, dma((atoms,)), dma((3, 4)), dma((3, 4)), dma((3, 2)), dma((3, 2)), dma((3, 2, 2)), dma((3, 2, 2)),
            dma((2, 3, 3)), dma((2, 3, 3)),
            *[dma((9,)) for _ in range(6)], *[dma((8,)) for _ in range(4)],
        ],
        compiler_params=pltpu.CompilerParams(
            collective_id=0, has_side_effects=True, vmem_limit_bytes=60 << 20
        ),
        cost_estimate=pl.CostEstimate(
            flops=2 * (atoms * size) ** 2 * points, bytes_accessed=20 << 20, transcendentals=0
        ),
    )(
        owner.reshape(1, -1), block.reshape(1, -1), pairs, weights.reshape(-1, size), basis,
        density, density_mask, inverse, inverse_mask,
    )


def local(
    basis_values,
    potential,
    pair_atoms,
    target_device,
    target_block,
    density,
    density_mask,
    inverse_intersection,
    inverse_mask,
):
    return gradient_tile(
        target_device,
        target_block,
        pair_atoms,
        potential,
        basis_values,
        density,
        density_mask,
        inverse_intersection,
        inverse_mask,
    )


def solution(mesh):
    placed = (
        P(ALL, None, None),
        P(ALL),
        P(None, ALL),
        P(ALL, None),
        P(ALL),
        P("row", "col"),
        P("row", "col"),
        P("row", "col"),
        P("row", "col"),
    )
    return jax.shard_map(
        local, mesh=mesh, in_specs=placed, out_specs=P("row", ("col", "panel")), check_vma=False
    )
```

```python
import functools

import jax
import jax.numpy as jnp
from jax import lax
from jax.experimental import pallas as pl
from jax.experimental.pallas import tpu as pltpu
from jax.sharding import PartitionSpec as P

ALL = ("row", "col", "panel")


SIZE = 128
SHARES = (48, 48, 32)
STARTS = (0, 48, 96)
ORDERS = (("x", "y", "z"), ("z", "x", "y"), ("y", "z", "x"))


def place():
    row, col, core = (lax.axis_index(axis) for axis in ALL)
    return {"x": col % 2 * 2 + row % 2, "y": row // 2, "z": col // 2, "core": core}


def device_at(spot):
    return (spot["y"] * 2 + spot["x"] % 2, spot["z"] * 2 + spot["x"] // 2, spot["core"])


def moved(spot, axis, steps):
    return {**spot, axis: (spot[axis] + steps) % (2 if axis == "core" else 4)}


def tile_column(spot):
    return spot["z"] * 2 + spot["x"] // 2


def tile_row(spot):
    return spot["y"] * 2 + spot["x"] % 2


STEPS = ((2, 1), (1, 1), (3, 1), (2, 0), (0, 1), (1, 0), (3, 0))


class Gather:
    def __init__(self, here, ring, mirror, view, send, recv):
        self.here, self.ring, self.mirror, self.view, self.send, self.recv = here, ring, mirror, view, send, recv

    def spot(self, steps, image):
        there = moved(self.here, self.ring, steps)
        x = there["x"]
        if image and self.mirror == "x_hi":
            x = (x + 2) % 4
        elif image:
            x = x // 2 * 2 + (x + 1) % 2
        return {**there, "x": x}

    def copy(self, ref, at, spot):
        return pltpu.make_async_remote_copy(
            src_ref=ref, dst_ref=ref, send_sem=self.send.at[at], recv_sem=self.recv.at[at],
            device_id=device_at(spot), device_id_type=pl.DeviceIdType.MESH,
        )

    def cross(self):
        return self.copy(self.view(self.here, None), 0, self.spot(0, 1))

    def hop(self, side, image):
        ref = self.view(self.spot(0, image), None)
        return self.copy(ref, 1 + side * 2 + image, self.spot(3 if side else 1, 0))

    def far(self, side, image):
        ref = self.view(self.spot(1 if side else 3, image), side)
        return self.copy(ref, 5 + side * 2 + image, self.spot(3 if side else 1, 0))

    def begin(self):
        self.cross().start()
        self.begin_ring()

    def begin_ring(self):
        self.hop(0, 0).start()
        self.hop(1, 0).start()

    def second(self):
        self.cross().wait_recv()
        for side in range(2):
            self.hop(side, 1).start()
        for side in range(2):
            self.hop(side, 0).wait_recv()
            self.far(side, 0).start()

    def third(self):
        for side in range(2):
            self.hop(side, 1).wait_recv()
            self.far(side, 1).start()

    def finish(self):
        for side in range(2):
            for image in range(2):
                self.far(side, image).wait_recv()

    def sent(self):
        self.cross().wait_send()
        for side in range(2):
            for image in range(2):
                self.hop(side, image).wait_send()
                self.far(side, image).wait_send()


def whole_kernel(
    owner_in, block_in, atoms_in, weight_in, basis_ref, density_in, density_mask_in, inverse_ref, inverse_mask_in, out_ref,
    owner_ref, block_ref, atoms_ref, weight_ref, density_ref, density_mask_ref, inverse_mask_ref, small_sem,
    table, index_ref, inverse_half, raw, left, right, blocks, column,
    own0, own1, own2, give0, give1, give2, pair0, pair1, pair2,
    relay0, relay1, relay2, near0, near1, near2, one0, one1, one2,
    got20, got21, got22, two0, two1, two2, got30, got31, got32,
    p_row, s_col, x_col, row_buf,
    table_sem, half_sem, fetch_sem, pair_send, pair_recv, relay_send, relay_recv, near_send, near_recv, send_sem, recv_sem,
    p_send, p_recv, s_send, s_recv, x_send, x_recv, gather_send, gather_recv, share_send, share_recv,
):
    here = place()
    own, give, pair = (own0, own1, own2), (give0, give1, give2), (pair0, pair1, pair2)
    relay, near, one = (relay0, relay1, relay2), (near0, near1, near2), (one0, one1, one2)
    two = (two0, two1, two2)
    sources, lands = (None, one, two), (None, (got20, got21, got22), (got30, got31, got32))
    partner = moved(here, "core", 1)
    mesh = pl.DeviceIdType.MESH
    atoms, points, size = basis_ref.shape
    chunks = points // size
    slots = raw.shape[0]

    def fetch(a):
        return pltpu.make_async_copy(basis_ref.at[a], raw.at[a % slots], fetch_sem.at[a])

    peers = [partner]
    for axis in ("x", "y", "z"):
        peers += [moved(here, axis, d) for d in (1, 2, 3)]
    peers += [moved(moved(here, "x", 2), "z", d) for d in (1, 2, 3)]
    barrier = pltpu.get_barrier_semaphore()
    for peer in peers:
        pl.semaphore_signal(barrier, inc=1, device_id=device_at(peer), device_id_type=mesh)

    tile = 2 * size
    half_cols = pl.ds(pl.multiple_of(here["core"] * tile, tile), tile)
    fetch_half = pltpu.make_async_copy(inverse_ref.at[:, half_cols], inverse_half, half_sem)
    fetch_half.start()
    small = [
        pltpu.make_async_copy(source, held, small_sem.at[i])
        for i, (source, held) in enumerate(
            (
                (weight_in, weight_ref), (owner_in, owner_ref), (block_in, block_ref), (atoms_in, atoms_ref),
                (density_in, density_ref), (density_mask_in, density_mask_ref), (inverse_mask_in, inverse_mask_ref),
            )
        )
    ]
    for copy in small:
        copy.start()
    for a in range(slots):
        fetch(a).start()

    for copy in small:
        copy.wait()
    for k in range(chunks):
        spread_row = jnp.broadcast_to(weight_ref[k : k + 1, :], (size, size))
        column[k * size : (k + 1) * size, :] = spread_row.T

    def upright(row):
        return jnp.broadcast_to(row, (size, size)).T

    count = owner_ref.shape[1]
    serial = lax.broadcasted_iota(jnp.int32, (1, count), 1)
    target = upright(owner_ref[...] * 2 + block_ref[...])
    key = upright((serial * atoms + atoms_ref[0:1, :]) * atoms + atoms_ref[1:2, :])
    lane = lax.broadcasted_iota(jnp.int32, (size, size), 1)
    for part in range(table.shape[1] // size):
        hit = target == lane + part * size
        low = jnp.min(jnp.where(hit, key, 1 << 30), axis=0, keepdims=True)
        high = jnp.max(jnp.where(hit, key, -1), axis=0, keepdims=True)
        cols = pl.ds(part * size, size)
        table[0:1, cols] = jnp.where(high >= 0, low % (atoms * atoms), atoms * atoms)
        table[1:2, cols] = jnp.where(high > low, high % (atoms * atoms), atoms * atoms)
    fetch_table = pltpu.make_async_copy(table, index_ref, table_sem)
    fetch_table.start()
    blocks[atoms * atoms] = jnp.zeros((size, size), jnp.bfloat16)

    def remote(src, dst, send, recv, spot):
        return pltpu.make_async_remote_copy(
            src_ref=src, dst_ref=dst, send_sem=send, recv_sem=recv,
            device_id=device_at(spot), device_id_type=mesh,
        )

    own_col = pl.ds(pl.multiple_of(tile_column(here) * tile, tile), tile)
    own_row = pl.ds(pl.multiple_of(tile_row(here) * tile, tile), tile)

    def p_view(spot, half):
        rows = pl.ds(0, tile) if half is None else pl.ds(half * size, size)
        return p_row.at[rows, pl.ds(pl.multiple_of(tile_column(spot) * tile, tile), tile)]

    def row_view(ref):
        def view(spot, half):
            start = tile_row(spot) * tile + (half or 0) * size
            return ref.at[pl.ds(pl.multiple_of(start, size), tile if half is None else size), :]

        return view

    p_all = Gather(here, "z", "x_hi", p_view, p_send, p_recv)
    s_all = Gather(here, "y", "x_lo", row_view(s_col), s_send, s_recv)
    x_all = Gather(here, "y", "x_lo", row_view(x_col), x_send, x_recv)

    def masked(block, keep):
        return (block.astype(jnp.float32) * keep.astype(jnp.float32)).astype(jnp.bfloat16)

    fetch_half.wait()
    for i in range(2):
        for j in range(2):
            rows, cols = pl.ds(i * size, size), pl.ds(j * size, size)
            own_rows = pl.ds(pl.multiple_of(tile_row(here) * tile + i * size, size), size)
            own_cols = pl.ds(pl.multiple_of(tile_column(here) * tile + j * size, size), size)
            p_row[rows, own_cols] = masked(density_ref[rows, cols], density_mask_ref[i, j])
            s_col[own_rows, cols] = masked(inverse_half[rows, cols], inverse_mask_ref[i, here["core"] * 2 + j])
    pl.semaphore_wait(barrier, len(peers))
    p_all.begin()
    s_all.begin()

    def prepare(a):
        fetch(a).wait()
        cols = pl.ds(a * size, size)
        for k in range(chunks):
            rows = pl.ds(k * size, size)
            piece = raw[a % slots, rows, :]
            left[cols, rows] = piece.T
            scaled = piece.astype(jnp.float32) * column[rows, :]
            right[rows, cols] = scaled.astype(jnp.bfloat16)
        if a < atoms - slots:
            fetch(a + slots).start()

    for a in range(atoms):
        prepare(a)
    for j in range(0, atoms, 2):
        cols = pl.ds(j * size, tile)
        product = jnp.dot(left[: (j + 2) * size, :], right[:, cols], preferred_element_type=jnp.float32)
        for u in range(j + 2):
            for v in range(2):
                part = product[u * size : (u + 1) * size, v * size : (v + 1) * size].astype(jnp.bfloat16)
                blocks[u * atoms + j + v] = part
                if u < j:
                    blocks[(j + v) * atoms + u] = part.T
        if j == 4:
            p_all.second()
            s_all.second()
        if j == 10:
            p_all.third()
            s_all.third()

    def spot_of(k, d):
        return (here[ORDERS[k][0]] + d) % 4

    def assembled(k, q, m, g, core, also=None):
        at = dict(zip(ORDERS[k], (q, m, g // 2)))
        n = ((tile_row(at) * 8 + tile_column(at)) * 2 + core) * 2 + g % 2
        rows = pl.ds(STARTS[k], SHARES[k])
        if also is None:
            return blocks[index_ref[0, n], rows, :] + blocks[index_ref[1, n], rows, :]
        total = blocks[index_ref[0, n], rows, :].astype(jnp.float32) + blocks[index_ref[1, n], rows, :].astype(jnp.float32)
        return (total + also.astype(jnp.float32)).astype(jnp.bfloat16)

    def swap(k, d):
        q = spot_of(k, d)
        return remote(give[k].at[q], pair[k].at[q], pair_send.at[k, d], pair_recv.at[k, d], partner)

    def pass_relay(k, side):
        half = pl.ds(16 * side, 16)
        return remote(
            own[k].at[spot_of(k, 2), half], relay[k].at[side], relay_send.at[k, side], relay_recv.at[k, side],
            moved(here, ORDERS[k][0], 3 if side else 1),
        )

    def pass_near(k, side, part):
        half = pl.ds(16 * part, 16)
        d = 3 if side else 1
        return remote(
            own[k].at[spot_of(k, d), half], near[k].at[side, half],
            near_send.at[k, side, part], near_recv.at[k, side, part], moved(here, ORDERS[k][0], d),
        )

    def pass_on(stage, k, d):
        axis = ORDERS[k][stage]
        return remote(
            sources[stage][k].at[(here[axis] + d) % 4], lands[stage][k].at[d - 1],
            send_sem.at[stage - 1, k, d - 1], recv_sem.at[stage - 1, k, d - 1], moved(here, axis, d),
        )

    def give_away(d):
        for k in range(3):
            q = spot_of(k, d)

            @pl.loop(0, 4)
            def _(m):
                for g in range(8):
                    give[k][q, m * 8 + g] = assembled(k, q, m, g, partner["core"])

            swap(k, d).start()

    def take_in(d):
        for k in range(3):
            q = spot_of(k, d)
            swap(k, d).wait_recv()

            @pl.loop(0, 4)
            def _(m):
                for g in range(8):
                    own[k][q, m * 8 + g] = assembled(k, q, m, g, here["core"], pair[k][q, m * 8 + g])

            if d == 2:
                pass_relay(k, 0).start()
                pass_relay(k, 1).start()
            if d == 1:
                pass_near(k, 0, 1).start()
            if d == 3:
                pass_near(k, 1, 0).start()

    def pass_relayed(side):
        for k in range(3):
            q = spot_of(k, 3 if side else 1)
            pass_relay(k, side).wait_recv()

            @pl.loop(0, 4)
            def _(m):
                for g in range(4):
                    n = m * 4 + g
                    own[k][q, 16 * side + n] = own[k][q, 16 * side + n] + relay[k][side, n]

            pass_near(k, side, side).start()

    turns = (2, 1, 3, 0)
    fetch_table.wait()
    give_away(2)
    give_away(1)
    take_in(2)
    give_away(3)
    take_in(1)
    give_away(0)
    p_all.finish()
    s_all.finish()
    x_col[own_row, :] = jnp.dot(p_row[...], s_col[...], preferred_element_type=jnp.float32).astype(jnp.bfloat16)
    take_in(3)
    x_all.begin_ring()
    pass_relayed(0)
    pass_relayed(1)
    take_in(0)
    for k in range(3):
        q = spot_of(k, 0)
        for side in range(2):
            for part in range(2):
                pass_near(k, side, part).wait_recv()

        for d in turns:
            m = (here[ORDERS[k][1]] + d) % 4
            for g in range(8):
                n = m * 8 + g
                total = own[k][q, n].astype(jnp.float32) + near[k][0, n].astype(jnp.float32)
                one[k][m, g] = (total + near[k][1, n].astype(jnp.float32)).astype(jnp.bfloat16)
            if d:
                pass_on(1, k, d).start()

    x_all.cross().start()

    def added(stage, k, n):
        mine = sources[stage][k][here[ORDERS[k][stage]], n].astype(jnp.float32)
        for d in range(3):
            mine = mine + lands[stage][k][d, n].astype(jnp.float32)
        return mine.astype(jnp.bfloat16)

    for k in range(3):
        for d in (1, 2, 3):
            pass_on(1, k, d).wait_recv()
        for d in turns:
            q = (here[ORDERS[k][2]] + d) % 4
            for b in range(2):
                two[k][q, b] = added(1, k, q * 2 + b)
            if d:
                pass_on(2, k, d).start()
    x_all.second()

    core_row = pl.multiple_of(here["core"] * size, size)
    for k in range(3):
        for d in (1, 2, 3):
            pass_on(2, k, d).wait_recv()
        for b in range(2):
            cols = pl.ds(pl.multiple_of(tile_column(here) * tile + b * size, size), size)
            row_buf[pl.ds(core_row + STARTS[k], SHARES[k]), cols] = added(2, k, b)

    def tile_of(steps, image):
        cols = pl.ds(pl.multiple_of(tile_column(p_all.spot(steps, image)) * tile, tile), tile)
        return row_buf.at[pl.ds(core_row, size), cols]

    def spread(steps, image):
        at = steps * 2 + image
        return remote(tile_of(0, 0), tile_of(0, 0), gather_send.at[at], gather_recv.at[at], p_all.spot(steps, image))

    def share(steps, image):
        ref = tile_of((4 - steps) % 4, image)
        at = steps * 2 + image
        return remote(ref, ref, share_send.at[at], share_recv.at[at], partner)

    for step in STEPS:
        spread(*step).start()
    share(0, 0).start()
    x_all.third()
    x_all.finish()
    for step in STEPS[::-1]:
        spread(*step).wait_recv()
        share(*step).start()
    def finish_rows(start):
        rows = pl.ds(pl.multiple_of(start, size), size)
        out_ref[rows, :] = jnp.dot(row_buf[rows, :], x_col[...], preferred_element_type=jnp.float32)

    finish_rows(core_row)
    for step in ((0, 0),) + STEPS:
        share(*step).wait_recv()
    finish_rows(size - core_row)

    for gather in (p_all, s_all, x_all):
        gather.sent()
    for step in STEPS:
        spread(*step).wait_send()
        share(*step).wait_send()
    share(0, 0).wait_send()
    for k in range(3):
        for d in turns:
            swap(k, d).wait_send()
        for side in range(2):
            pass_relay(k, side).wait_send()
            for part in range(2):
                pass_near(k, side, part).wait_send()
        for stage in (1, 2):
            for d in (1, 2, 3):
                pass_on(stage, k, d).wait_send()


def gradient_tile(owner, block, pairs, weights, basis, density, density_mask, inverse, inverse_mask):
    atoms, points, size = basis.shape
    depth = 16 * size

    def buffers(*lead):
        return [pltpu.VMEM((*lead, share, size), jnp.bfloat16) for share in SHARES]

    def plain(*shape):
        return pltpu.VMEM(shape, jnp.bfloat16)

    dma = pltpu.SemaphoreType.DMA
    vmem = pl.BlockSpec(memory_space=pltpu.VMEM)
    hbm = pl.BlockSpec(memory_space=pl.ANY)
    return pl.pallas_call(
        whole_kernel,
        out_shape=jax.ShapeDtypeStruct((2 * size, 2 * size), jnp.float32),
        in_specs=[hbm] * 9,
        out_specs=vmem,
        scratch_shapes=[
            pltpu.VMEM((1, owner.shape[0]), jnp.int32), pltpu.VMEM((1, owner.shape[0]), jnp.int32),
            pltpu.VMEM(pairs.shape, jnp.int32), pltpu.VMEM((points // size, size), jnp.float32),
            plain(*density.shape), pltpu.SMEM(density_mask.shape, jnp.int32), pltpu.SMEM(inverse_mask.shape, jnp.int32),
            dma((7,)),
            pltpu.VMEM((2, 2 * size), jnp.int32), pltpu.SMEM((2, 2 * size), jnp.int32), plain(2 * size, 2 * size),
            plain(atoms // 2, points, size), plain(atoms * size, points), plain(points, atoms * size),
            plain(atoms * atoms + 1, size, size), pltpu.VMEM((points, size), jnp.float32),
            *buffers(4, 32), *buffers(4, 32), *buffers(4, 32),
            *buffers(2, 16), *buffers(2, 32), *buffers(4, 8),
            *buffers(3, 8), *buffers(4, 2), *buffers(3, 2),
            plain(2 * size, depth), plain(depth, 2 * size), plain(depth, 2 * size), plain(2 * size, depth),
            dma, dma, dma((atoms,)), dma((3, 4)), dma((3, 4)), dma((3, 2)), dma((3, 2)), dma((3, 2, 2)), dma((3, 2, 2)),
            dma((2, 3, 3)), dma((2, 3, 3)),
            *[dma((9,)) for _ in range(6)], *[dma((8,)) for _ in range(4)],
        ],
        compiler_params=pltpu.CompilerParams(
            collective_id=0, has_side_effects=True, vmem_limit_bytes=60 << 20
        ),
        cost_estimate=pl.CostEstimate(
            flops=2 * (atoms * size) ** 2 * points, bytes_accessed=20 << 20, transcendentals=0
        ),
    )(
        owner.reshape(1, -1), block.reshape(1, -1), pairs, weights.reshape(-1, size), basis,
        density, density_mask, inverse, inverse_mask,
    )


def local(
    basis_values,
    potential,
    pair_atoms,
    target_device,
    target_block,
    density,
    density_mask,
    inverse_intersection,
    inverse_mask,
):
    return gradient_tile(
        target_device,
        target_block,
        pair_atoms,
        potential,
        basis_values,
        density,
        density_mask,
        inverse_intersection,
        inverse_mask,
    )


def solution(mesh):
    placed = (
        P(ALL, None, None),
        P(ALL),
        P(None, ALL),
        P(ALL, None),
        P(ALL),
        P("row", "col"),
        P("row", "col"),
        P("row", "col"),
        P("row", "col"),
    )
    return jax.shard_map(
        local, mesh=mesh, in_specs=placed, out_specs=P("row", ("col", "panel")), check_vma=False
    )
```
